512 devices in a mesh: sample: 32 (over z_lo, y), tok: 16 (over z_hi, x, core).
Axes of the slice: x: 4, y: 4, z: 16 (z_hi: 2, z_lo: 8; z = z_hi * 8 + z_lo), core: 2. Of those that a mesh axis runs over, the one named last changes fastest.
Arguments:
- noisy_tokens: bfloat16 [32, 512, 768], P('sample', 'tok'), may hold values from -6 to 6
- pair_bias: bfloat16 [16, 512, 512], P(None, 'tok', 'sample'), may hold values from -3 to 305
- chain_ids: int32 [512], replicated, may hold values from 0 to 7, never falling along the last dimension, each value on 1 to 128 neighbouring positions
- pad_mask: int32 [512], replicated, may hold values 0 or 1
- step_index: int32 [32], P('sample'), may hold values from 0 to 199
- chain_gain: float32 [16], replicated, may hold values from -3 to 3
- w_query: bfloat16 [768, 768], replicated, may hold values from -0.21875 to 0.21875
- w_key: bfloat16 [768, 768], replicated, may hold values from -0.21875 to 0.21875
- w_value: bfloat16 [768, 768], replicated, may hold values from -0.21875 to 0.21875
- w_output: bfloat16 [768, 768], replicated, may hold values from -0.21875 to 0.21875
Outputs:
- denoised: bfloat16 [32, 512, 768], P('sample', 'tok')
The draws below stay inside these ranges and needn't reach their ends.
Inputs may be any that keep to these rules, and one draw needn't show every extreme that they name: `chain_ids`: chains are contiguous runs of 1 to 128 tokens, numbered in order.
All inputs are finite; a program needn't handle non-finite values.
Results may differ from the reference program's by a relative error of at most 0.0034.
Values may be sent and summed in bfloat16 or wider, within the bound.
A program may use at most 64 MiB of HBM per device.

```python
import math
import jax
import jax.numpy as jnp
import numpy as np
from jax import lax

D = 768
H = 16
STEPS = 200
CHAINS = 8
N = 512
SAMPLES = 32


def draw_pair_bias(key, part):
    key = jax.random.fold_in(key, 11)
    keys = jax.random.split(key, 1)
    shape = (H, N, N)
    values = 0.75 * jax.random.truncated_normal(keys[0], -4.0, 4.0, shape, jnp.float32)
    return values.astype(jnp.bfloat16)


def with_ends(drawn, rng, low, high):
    dims = drawn.shape
    place = [jax.random.randint(jax.random.fold_in(rng, axis), (), 0, dims[axis]) for axis in range(len(dims))]
    drawn = drawn.at[tuple(place)].set(low)
    longest = dims.index(max(dims))
    place[longest] = (place[longest] + 1) % dims[longest]
    return drawn.at[tuple(place)].set(high)


def steps_of(rng, dims, pieces, low, high):
    factor_of, own = 1.0, jax.random.fold_in(rng, 6)
    for axis_at, parts in pieces:
        draws = jnp.exp(jax.random.uniform(jax.random.fold_in(own, axis_at), (parts,), jnp.float32, low / len(pieces), high / len(pieces)))
        factor_of = factor_of * jnp.repeat(draws, dims[axis_at] // parts).reshape([-1 if axis == axis_at else 1 for axis in range(len(dims))])
    return factor_of


def profile(count, total, limit, lean):
    portions = [(1 << 20) // math.isqrt(rank ** lean) + 1 for rank in range(2, count + 1)]
    surplus, holding = total - limit - (count - 1), [1] * (count - 1)
    while surplus > 0:
        movable = [i for i in range(count - 1) if holding[i] < limit]
        pool, remaining = sum([portions[i] for i in movable]), surplus
        for i in movable:
            more = min(limit - holding[i], max(1, remaining * portions[i] // pool), surplus)
            holding[i] = holding[i] + more
            surplus = surplus - more
    return np.array([limit] + holding)


def uneven(stream_key, number_of, total, bound, skew):
    if number_of == 2:
        one = jax.random.randint(stream_key, (), max(1, total - bound), min(bound, total - 1) + 1)
        return jnp.stack([one, total - one])
    tallies = jnp.asarray(profile(number_of, total, bound, skew), jnp.int32)
    twos = (number_of - 1) // 2
    source_of, taker = tallies[1:1 + 2 * twos:2], tallies[2:2 + 2 * twos:2]
    margin = jnp.minimum(source_of - 1, bound - taker)
    shifted = jax.random.randint(jax.random.fold_in(stream_key, 1), (twos,), 0, 1 << 20) % (margin + 1)
    tallies = tallies.at[1:1 + 2 * twos:2].set(source_of - shifted).at[2:2 + 2 * twos:2].set(taker + shifted)
    return tallies[jax.random.permutation(jax.random.fold_in(stream_key, 2), number_of)]


def bell_draw(own_key, shape, deviation, limit, cuts=(), kind=jnp.bfloat16):
    level = steps_of(own_key, shape, cuts, -0.22, 0.18) if cuts else 1.0
    result = jax.random.normal(own_key, shape, jnp.float32) * deviation * level
    return jnp.minimum(jnp.maximum(result, -limit), limit).astype(kind)


def setup_inputs(seed: int = 0) -> dict:
    splits = jax.random.split(jax.random.key(seed), 11)
    return {
        "noisy_tokens": bell_draw(splits[0], (SAMPLES, N, D), 1.0, 6.0, ((0, 32), (1, 16))),
        "pair_bias": draw_pair_bias(jax.random.fold_in(splits[10], 71), 0),
        "chain_ids": jnp.searchsorted(jnp.cumsum(uneven(splits[2], CHAINS, N, N // 4, 0)), jnp.arange(N), side="right").astype(jnp.int32),
        "pad_mask": with_ends((jax.random.randint(splits[3], (N,), 0, 8) < 7).astype(jnp.int32), jax.random.fold_in(splits[3], 1), 0, 1),
        "step_index": with_ends(jax.random.randint(splits[4], (SAMPLES,), 0, STEPS), jax.random.fold_in(splits[4], 1), 0, STEPS - 1).astype(jnp.int32),
        "chain_gain": jnp.clip(jax.random.uniform(splits[5], (H,), jnp.float32, -3.0, 3.0), -3.0, 3.0),
        "w_query": bell_draw(splits[6], (D, D), D ** -0.5, 0.21875),
        "w_key": bell_draw(splits[7], (D, D), D ** -0.5, 0.21875),
        "w_value": bell_draw(splits[8], (D, D), D ** -0.5, 0.21875),
        "w_output": bell_draw(splits[9], (D, D), D ** -0.5, 0.21875),
    }


sigma_data = 16.0
sigma_top = 160.0
sigma_low = 0.0004
rho_exp = 7.0

def layer_norm(values):
    xf = values.astype(jnp.float32)
    center = xf - lax.optimization_barrier(jnp.mean(xf, axis=-1, keepdims=True))
    spread = lax.optimization_barrier(jnp.mean(center * center, axis=-1, keepdims=True))
    return (center * lax.rsqrt(spread + 1e-05)).astype(jnp.bfloat16)

def noise_factors(step_index):
    ratio = step_index.astype(jnp.float32) / (STEPS - 1)
    upper = sigma_top ** (1.0 / rho_exp)
    lower = sigma_low ** (1.0 / rho_exp)
    sigma = sigma_data * (upper + ratio * (lower - upper)) ** rho_exp
    skip_scale = sigma_data ** 2 / (sigma_data ** 2 + sigma * sigma)
    out_scale = sigma / jnp.sqrt(sigma * sigma + sigma_data ** 2)
    return (skip_scale, out_scale)

def reference(noisy_tokens, pair_bias, chain_ids, pad_mask, step_index, chain_gain, w_query, w_key, w_value, w_output):
    head_size = D // H
    same_chain = (chain_ids[:, None] == chain_ids[None, :]).astype(jnp.float32)
    masked = (pad_mask.astype(jnp.float32) - 1.0) * 1000000000.0
    bias_full = pair_bias.astype(jnp.float32)

    def one_sample(items):
        tokens, step = items
        normed = layer_norm(tokens)
        queries = jnp.dot(normed, w_query, preferred_element_type=jnp.float32).astype(jnp.bfloat16)
        key_rows = jnp.dot(normed, w_key, preferred_element_type=jnp.float32).astype(jnp.bfloat16)
        value_rows = jnp.dot(normed, w_value, preferred_element_type=jnp.float32).astype(jnp.bfloat16)
        query_heads = queries.reshape(N, H, head_size).astype(jnp.float32)
        key_heads = key_rows.reshape(N, H, head_size).astype(jnp.float32)
        value_heads = value_rows.reshape(N, H, head_size).astype(jnp.float32)
        scores = jnp.einsum('ihd,jhd->hij', query_heads, key_heads) / jnp.sqrt(jnp.float32(head_size))
        scores = scores + bias_full + chain_gain[:, None, None] * same_chain[None] + masked[None, None, :]
        top = lax.optimization_barrier(jnp.max(scores, axis=-1, keepdims=True))
        expo = jnp.exp(scores - top)
        weights = (expo / lax.optimization_barrier(jnp.sum(expo, axis=-1, keepdims=True))).astype(jnp.bfloat16)
        attended = jnp.einsum('hij,jhd->ihd', weights.astype(jnp.float32), value_heads)
        attended = attended.reshape(N, D).astype(jnp.bfloat16)
        projected = jnp.dot(attended, w_output, preferred_element_type=jnp.float32)
        skip_scale, out_scale = noise_factors(step)
        return (skip_scale * tokens.astype(jnp.float32) + out_scale * projected).astype(jnp.bfloat16)
    return lax.map(one_sample, (noisy_tokens, step_index))
```

```python
import functools
import math

import jax
import jax.numpy as jnp
from jax import lax
from jax.experimental import pallas as pl
from jax.experimental.pallas import tpu as pltpu
from jax.sharding import PartitionSpec as P

STEPS = 200
SIGMA_DATA = 16.0
SIGMA_TOP = 160.0
SIGMA_LOW = 0.0004
RHO = 7

Y, Z_LO = 4, 8
X, CORES = 4, 2

MESH = pl.DeviceIdType.MESH
F32 = jnp.float32
BF16 = jnp.bfloat16
NEAR = (Z_LO - 1) + (Y - 1) + (X - 1) + (CORES - 1)


def dot(a, b):
    return lax.dot_general(a, b, (((1,), (0,)), ((), ())), preferred_element_type=F32)


def dot_t(a, b):
    return lax.dot_general(a, b, (((1,), (1,)), ((), ())), preferred_element_type=F32)


def kernel(
    x_hbm, bias_hbm, chain_hbm, pad_hbm, step_hbm, gain_hbm, wq_hbm, wk_hbm, wv_hbm, wo_hbm,
    out_ref,
    x_raw, bias_raw, chain_v, pad_v, step_s, gain_s, wq, wk, wv, wo,
    xbuf, bbuf, kbuf, vbuf, qexp, wvt, ebuf, chain_col, mask_col,
    lsem, xs, xr, bzs, bzr, bys, byr, ready,
):
    heads, keys_each, rows = bias_hbm.shape
    width = x_hbm.shape[2]
    half = xbuf.shape[0] // 2
    head_size = width // heads
    lanes = heads * rows

    s, t = lax.axis_index("sample"), lax.axis_index("tok")
    y, zl = s % Y, s // Y
    core, cx, zh = t % CORES, (t // CORES) % X, t // (CORES * X)

    def tok_of(h, x, c):
        return h * (X * CORES) + x * CORES + c

    def other_x(k):
        return (cx + k) % X

    far = (s, tok_of(1 - zh, cx, core))
    sibling = (s, tok_of(zh, cx, 1 - core))
    along_x = [(s, tok_of(zh, other_x(k), core)) for k in range(1, X)]
    along_y = [(zl * Y + (y + k) % Y, t) for k in range(1, Y)]
    along_z = [(((zl + k) % Z_LO) * Y + y, t) for k in range(1, Z_LO)]

    barrier = pltpu.get_barrier_semaphore()

    @pl.when(zh == 0)
    def _():
        pl.semaphore_signal(barrier, inc=1, device_id=far, device_id_type=MESH)

    for who in along_x + [sibling] + along_z + along_y:
        pl.semaphore_signal(barrier, inc=1, device_id=who, device_id_type=MESH)

    loads = [
        pltpu.make_async_copy(src, dst, lsem.at[n])
        for n, (src, dst) in enumerate(
            [
                (x_hbm, x_raw), (bias_hbm, bias_raw), (chain_hbm, chain_v), (pad_hbm, pad_v),
                (step_hbm, step_s), (gain_hbm, gain_s), (wq_hbm, wq), (wk_hbm, wk), (wv_hbm, wv), (wo_hbm, wo),
            ]
        )
    ]
    for load in loads:
        load.start()

    loads[0].wait()
    xf = x_raw[0].astype(F32)
    center = xf - jnp.mean(xf, axis=-1, keepdims=True)
    spread = jnp.mean(center * center, axis=-1, keepdims=True)
    xbuf[t] = (center * lax.rsqrt(spread + 1e-05)).astype(BF16)

    loads[1].wait()
    bbuf[zl, y] = jnp.concatenate([bias_raw[h] for h in range(heads)], axis=1)

    pl.semaphore_wait(barrier, NEAR + zh)

    def send_x(block, n, who):
        copy = pltpu.make_async_remote_copy(
            src_ref=xbuf.at[block], dst_ref=xbuf.at[block], send_sem=xs.at[n], recv_sem=xr.at[block],
            device_id=who, device_id_type=MESH,
        )
        copy.start()
        return copy

    def recv_x(block):
        pltpu.make_async_remote_copy(
            src_ref=xbuf.at[block], dst_ref=xbuf.at[block], send_sem=xs.at[0], recv_sem=xr.at[block],
            device_id=sibling, device_id_type=MESH,
        ).wait_recv()

    sent = []

    @pl.when(zh == 1)
    def _():
        send_x(t, 0, far)
        pl.semaphore_signal(ready, inc=1, device_id=far, device_id_type=MESH)

    sent += [send_x(t, 1 + k, along_x[k]) for k in range(X - 1)]
    sent.append(send_x(t, X, sibling))
    for k, who in enumerate(along_z):
        copy = pltpu.make_async_remote_copy(
            src_ref=bbuf.at[zl, y], dst_ref=bbuf.at[zl, y], send_sem=bzs.at[k], recv_sem=bzr.at[zl],
            device_id=who, device_id_type=MESH,
        )
        copy.start()
        sent.append(copy)

    loads[2].wait()
    loads[3].wait()
    tokens = chain_v.shape[0]
    chain_row = chain_v[...].astype(F32).reshape(1, tokens)
    chain_col[...] = jnp.transpose(jnp.broadcast_to(chain_row, (128, tokens)))
    mask_row = (pad_v[...].astype(F32).reshape(1, tokens) - 1.0) * 1000000000.0
    mask_col[...] = jnp.transpose(jnp.broadcast_to(mask_row, (128, tokens)))
    lane = lax.broadcasted_iota(jnp.int32, (rows, lanes), 1)
    query = lax.broadcasted_iota(jnp.int32, (rows, lanes), 0)
    pick = lane % rows == query
    own_chain = chain_col[pl.ds(pl.multiple_of(t * rows, rows), rows), 0:1]
    query_chain = jnp.sum(jnp.where(pick, own_chain, 0.0), axis=0, keepdims=True)
    loads[4].wait()
    loads[5].wait()
    gain = jnp.zeros((1, lanes), F32)
    lane_head = lax.broadcasted_iota(jnp.int32, (1, lanes), 1) // rows
    for h in range(heads):
        gain = jnp.where(lane_head == h, gain_s[h], gain)

    loads[6].wait()
    queries = dot(xbuf[t], wq[...]).astype(BF16)
    group_heads = heads // 2
    group_width = width // 2
    group_lanes = lanes // 2
    row_head = lax.broadcasted_iota(jnp.int32, (group_lanes, group_width), 0) // rows
    col_head = lax.broadcasted_iota(jnp.int32, (group_lanes, group_width), 1) // head_size
    for g in range(2):
        part = queries[:, g * group_width : (g + 1) * group_width]
        tiled = jnp.concatenate([part] * group_heads, axis=0)
        qexp[g] = jnp.where(row_head == col_head, tiled, jnp.zeros_like(tiled))

    loads[7].wait()
    loads[8].wait()
    wvt[...] = jnp.transpose(wv[...])

    def keys_values(n, which):
        block = xbuf[pl.ds(which * half, half)].reshape(half * rows, width)
        kbuf[n] = dot(block, wk[...]).astype(BF16)
        vbuf[n] = dot_t(wvt[...], block).astype(BF16)

    def scores(n, which):
        first = pl.multiple_of(which * (half * rows), half * rows)
        z_half = which * (Z_LO // 2)
        key = kbuf[n]
        found = jnp.concatenate(
            [dot_t(key[:, g * group_width : (g + 1) * group_width], qexp[g]) for g in range(2)], axis=1
        )
        bias = bbuf[pl.ds(z_half, Z_LO // 2)].reshape(half * rows, lanes).astype(F32)
        same = chain_col[pl.ds(first, half * rows), 0:1] == query_chain
        found = found * (1.0 / math.sqrt(head_size)) + bias
        found = found + jnp.where(same, gain, 0.0)
        found = found + mask_col[pl.ds(first, half * rows), 0:1]
        top = jnp.max(found, axis=0, keepdims=True)
        expo = jnp.exp(found - top)
        ebuf[n] = expo
        return top, jnp.sum(expo, axis=0, keepdims=True)

    for k in range(1, X):
        block = tok_of(zh, other_x(k), core)
        recv_x(block)
        sent.append(send_x(block, X + k, sibling))
    for k in range(X):
        recv_x(tok_of(zh, other_x(k), 1 - core))
    keys_values(0, zh)

    for k in range(1, Z_LO):
        there = (zl + k) % Z_LO
        pltpu.make_async_remote_copy(
            src_ref=bbuf.at[zl, y], dst_ref=bbuf.at[there, y], send_sem=bzs.at[0], recv_sem=bzr.at[there],
            device_id=sibling, device_id_type=MESH,
        ).wait_recv()
    for k, who in enumerate(along_y):
        copy = pltpu.make_async_remote_copy(
            src_ref=bbuf.at[:, y], dst_ref=bbuf.at[:, y], send_sem=bys.at[k], recv_sem=byr.at[y],
            device_id=who, device_id_type=MESH,
        )
        copy.start()
        sent.append(copy)

    @pl.when(zh == 0)
    def _():
        pl.semaphore_wait(ready, 1)
        send_x(t, 0, far)

    block = tok_of(1 - zh, cx, core)
    recv_x(block)
    for k in range(X - 1):
        sent.append(send_x(block, 2 * X + k, along_x[k]))
    sent.append(send_x(block, 3 * X - 1, sibling))

    for k in range(1, Y):
        there = (y + k) % Y
        pltpu.make_async_remote_copy(
            src_ref=bbuf.at[:, y], dst_ref=bbuf.at[:, there], send_sem=bys.at[0], recv_sem=byr.at[there],
            device_id=sibling, device_id_type=MESH,
        ).wait_recv()
    top_0, sum_0 = scores(0, zh)

    for k in range(1, X):
        block = tok_of(1 - zh, other_x(k), core)
        recv_x(block)
        sent.append(send_x(block, 3 * X + k - 1, sibling))
    for k in range(X):
        recv_x(tok_of(1 - zh, other_x(k), 1 - core))
    keys_values(1, 1 - zh)
    top_1, sum_1 = scores(1, 1 - zh)

    top = jnp.maximum(top_0, top_1)
    part_0, part_1 = jnp.exp(top_0 - top), jnp.exp(top_1 - top)
    total = sum_0 * part_0 + sum_1 * part_1
    w_0 = (ebuf[0] * (part_0 / total)).astype(BF16)
    w_1 = (ebuf[1] * (part_1 / total)).astype(BF16)

    feature_head = lax.broadcasted_iota(jnp.int32, (group_width, group_lanes), 0) // head_size
    lane_of = lax.broadcasted_iota(jnp.int32, (group_width, group_lanes), 1) // rows
    place = pick[:, :group_lanes].astype(BF16)
    pieces = []
    for g in range(2):
        f = slice(g * group_width, (g + 1) * group_width)
        l = slice(g * group_lanes, (g + 1) * group_lanes)
        got = dot(vbuf[0, f, :], w_0[:, l]) + dot(vbuf[1, f, :], w_1[:, l])
        kept = jnp.where(feature_head == lane_of, got, 0.0).astype(BF16)
        pieces.append(dot_t(place, kept).astype(BF16))
    attended = jnp.concatenate(pieces, axis=1)

    loads[9].wait()
    projected = dot(attended, wo[...])
    ratio = jnp.full((1, width), step_s[0], jnp.int32).astype(F32) / (STEPS - 1)
    upper, lower = SIGMA_TOP ** (1.0 / RHO), SIGMA_LOW ** (1.0 / RHO)
    base = upper + ratio * (lower - upper)
    square = base * base
    sigma = SIGMA_DATA * (square * square * square * base)
    skip_scale = SIGMA_DATA**2 / (SIGMA_DATA**2 + sigma * sigma)
    out_scale = sigma / jnp.sqrt(sigma * sigma + SIGMA_DATA**2)
    out_ref[0] = (skip_scale * x_raw[0].astype(F32) + out_scale * projected).astype(BF16)

    for copy in sent:
        copy.wait_send()
    pltpu.make_async_remote_copy(
        src_ref=xbuf.at[t], dst_ref=xbuf.at[t], send_sem=xs.at[0], recv_sem=xr.at[t],
        device_id=far, device_id_type=MESH,
    ).wait_send()


def shards(noisy, pair_bias, chain_ids, pad_mask, step_index, chain_gain, w_query, w_key, w_value, w_output):
    samples, rows, width = noisy.shape
    heads, _, keys_each = pair_bias.shape
    tokens = chain_ids.shape[0]
    blocks = tokens // rows
    lanes = heads * rows
    half_rows = tokens // 2
    dma = pltpu.SemaphoreType.DMA
    weight = pltpu.VMEM((width, width), BF16)
    return pl.pallas_call(
        kernel,
        out_shape=jax.ShapeDtypeStruct((samples, rows, width), BF16),
        in_specs=[pl.BlockSpec(memory_space=pltpu.HBM)] * 10,
        out_specs=pl.BlockSpec(memory_space=pltpu.VMEM),
        scratch_shapes=[
            pltpu.VMEM((samples, rows, width), BF16),
            pltpu.VMEM((heads, keys_each, rows), BF16),
            pltpu.VMEM((tokens,), jnp.int32),
            pltpu.VMEM((tokens,), jnp.int32),
            pltpu.SMEM((1,), jnp.int32),
            pltpu.SMEM((heads,), F32),
            weight, weight, weight, weight,
            pltpu.VMEM((blocks, rows, width), BF16),
            pltpu.VMEM((Z_LO, Y, keys_each, lanes), BF16),
            pltpu.VMEM((2, half_rows, width), BF16),
            pltpu.VMEM((2, width, half_rows), BF16),
            pltpu.VMEM((2, lanes // 2, width // 2), BF16),
            weight,
            pltpu.VMEM((2, half_rows, lanes), F32),
            pltpu.VMEM((tokens, 128), F32),
            pltpu.VMEM((tokens, 128), F32),
            dma((10,)),
            dma((4 * X,)),
            dma((blocks,)),
            dma((Z_LO,)),
            dma((Z_LO,)),
            dma((Y,)),
            dma((Y,)),
            pltpu.SemaphoreType.REGULAR,
        ],
        compiler_params=pltpu.CompilerParams(
            collective_id=0, has_side_effects=True, vmem_limit_bytes=56 * 1024 * 1024
        ),
    )(
        noisy, jnp.transpose(pair_bias, (0, 2, 1)), chain_ids, pad_mask, step_index, chain_gain,
        w_query, w_key, w_value, w_output,
    )


def solution(mesh):
    in_specs = (
        P("sample", "tok", None),
        P(None, "tok", "sample"),
        P(),
        P(),
        P("sample"),
        P(),
        P(),
        P(),
        P(),
        P(),
    )
    out_specs = P("sample", "tok", None)
    return jax.shard_map(shards, mesh=mesh, in_specs=in_specs, out_specs=out_specs, check_vma=False)
```

```python
import functools
import math

import jax
import jax.numpy as jnp
from jax import lax
from jax.experimental import pallas as pl
from jax.experimental.pallas import tpu as pltpu
from jax.sharding import PartitionSpec as P

STEPS = 200
SIGMA_DATA = 16.0
SIGMA_TOP = 160.0
SIGMA_LOW = 0.0004
RHO = 7

Y, Z_LO = 4, 8
X, CORES = 4, 2

MESH = pl.DeviceIdType.MESH
F32 = jnp.float32
BF16 = jnp.bfloat16
QUAD = Z_LO // 2


def dot(a, b):
    return lax.dot_general(a, b, (((1,), (0,)), ((), ())), preferred_element_type=F32)


def dot_t(a, b):
    return lax.dot_general(a, b, (((1,), (1,)), ((), ())), preferred_element_type=F32)


def kernel(
    step_s, x_hbm, bias_hbm, chain_hbm, pad_hbm, gain_hbm, wq_hbm, wk_hbm, wv_hbm, wo_hbm,
    out_ref,
    x_raw, bias_raw, chain_v, pad_v, gain_s, wq, wk, wv, wo,
    xbuf, bbuf, kbuf, vbuf, qexp, wvt, ebuf, wbuf, chain_col, mask_col,
    lsem, xs, xr, bzs, bzr, bys, byr, ready_x, ready_core, ready_y, ready_near, ready_cross, ready_far,
):
    heads, keys_each, rows = bias_hbm.shape
    width = x_hbm.shape[2]
    per_half = xbuf.shape[0] // 2
    half = per_half * rows
    quarter = half // CORES
    head_size = width // heads
    lanes = heads * rows

    s, t = lax.axis_index("sample"), lax.axis_index("tok")
    y, zl = s % Y, s // Y
    core, cx, zh = t % CORES, (t // CORES) % X, t // (CORES * X)
    quad, place_z = zl // QUAD, zl % QUAD
    late = quad

    def tok_of(h, x, c):
        return h * (X * CORES) + x * CORES + c

    def block_of(h, x, c):
        return h * per_half + c * X + x

    def other_x(k):
        return (cx + k) % X

    far = (s, tok_of(1 - zh, cx, core))
    sibling = (s, tok_of(zh, cx, 1 - core))
    along_x = [(s, tok_of(zh, other_x(k), core)) for k in range(1, X)]
    along_x_both = [(s, tok_of(zh, other_x(k), c)) for k in range(1, X) for c in (core, 1 - core)]
    along_y = [(zl * Y + (y + k) % Y, t) for k in range(1, Y)]
    in_quad = [((quad * QUAD + (place_z + k) % QUAD) * Y + y, t) for k in range(1, QUAD)]
    opposite_z = (1 - quad) * QUAD + place_z
    opposite = (opposite_z * Y + y, t)

    def signal(semaphore, who):
        pl.semaphore_signal(semaphore, inc=1, device_id=who, device_id_type=MESH)

    barrier = pltpu.get_barrier_semaphore()

    @pl.when(zh == 0)
    def _():
        signal(barrier, far)

    @pl.when(core == CORES - 1)
    def _():
        signal(barrier, sibling)

    for k in range(1, X):

        @pl.when(cx + k < X)
        def _(k=k):
            signal(barrier, along_x[k - 1])

    for k in range(1, Y):

        @pl.when(y + k < Y)
        def _(k=k):
            signal(barrier, along_y[k - 1])

    for k in range(1, QUAD):

        @pl.when(place_z + k < QUAD)
        def _(k=k):
            signal(barrier, in_quad[k - 1])

    @pl.when(late == 0)
    def _():
        signal(barrier, opposite)

    loads = [
        pltpu.make_async_copy(src, dst, lsem.at[n])
        for n, (src, dst) in enumerate(
            [
                (x_hbm, x_raw), (bias_hbm, bias_raw), (chain_hbm, chain_v), (pad_hbm, pad_v),
                (gain_hbm, gain_s), (wq_hbm, wq), (wk_hbm, wk), (wv_hbm, wv), (wo_hbm, wo),
            ]
        )
    ]
    for load in loads:
        load.start()

    own = block_of(zh, cx, core)
    loads[0].wait()
    xf = x_raw[0].astype(F32)
    center = xf - jnp.mean(xf, axis=-1, keepdims=True)
    spread = jnp.mean(center * center, axis=-1, keepdims=True)
    xbuf[own] = (center * lax.rsqrt(spread + 1e-05)).astype(BF16)

    loads[1].wait()
    bbuf[zl, y] = jnp.concatenate([bias_raw[h] for h in range(heads)], axis=1)

    earlier = zh + (CORES - 1 - core) + cx + y + place_z + late

    @pl.when(earlier > 0)
    def _():
        pl.semaphore_wait(barrier, earlier)

    def x_copy(block, n, who):
        return pltpu.make_async_remote_copy(
            src_ref=xbuf.at[block], dst_ref=xbuf.at[block], send_sem=xs.at[n], recv_sem=xr.at[block],
            device_id=who, device_id_type=MESH,
        )

    def send_x(block, n, who):
        copy = x_copy(block, n, who)
        copy.start()
        return copy

    def recv_x(block):
        x_copy(block, 0, sibling).wait_recv()

    def z_copy(n, who, there=None):
        there = zl if there is None else there
        block = bbuf.at[there, y]
        return pltpu.make_async_remote_copy(
            src_ref=block, dst_ref=block, send_sem=bzs.at[n], recv_sem=bzr.at[there],
            device_id=who, device_id_type=MESH,
        )

    def y_copy(n, part, who, there):
        q = (quad + part) % 2
        return pltpu.make_async_remote_copy(
            src_ref=bbuf.at[pl.ds(q * QUAD, QUAD), y], dst_ref=bbuf.at[pl.ds(q * QUAD, QUAD), there],
            send_sem=bys.at[part * Y + n], recv_sem=byr.at[part * Y + there],
            device_id=who, device_id_type=MESH,
        )

    def hand_on_y(part):
        copies = [y_copy(n, part, who, y) for n, who in enumerate(along_y)]
        for copy in copies:
            copy.start()
        return copies

    @pl.when(zh == 1)
    def _():
        signal(ready_far, far)
        x_copy(own, 0, far).start()

    for k in range(1, X):

        @pl.when(cx + k >= X)
        def _(k=k):
            signal(ready_x, along_x[k - 1])
            x_copy(own, k, along_x[k - 1]).start()

    @pl.when(core == 0)
    def _():
        signal(ready_core, sibling)
        x_copy(own, X, sibling).start()

    for k in range(1, Y):

        @pl.when(y + k >= Y)
        def _(k=k):
            signal(ready_y, along_y[k - 1])

    for k in range(1, QUAD):

        @pl.when(place_z + k >= QUAD)
        def _(k=k):
            signal(ready_near, in_quad[k - 1])
            z_copy(k, in_quad[k - 1]).start()

    @pl.when(late == 1)
    def _():
        signal(ready_cross, opposite)
        z_copy(QUAD, opposite).start()

    @pl.when(core == CORES - 1)
    def _():
        pl.semaphore_wait(ready_core, 1)
        x_copy(own, X, sibling).start()

    @pl.when(cx < X - 1)
    def _():
        pl.semaphore_wait(ready_x, X - 1 - cx)

    for k in range(1, X):

        @pl.when(cx + k < X)
        def _(k=k):
            x_copy(own, k, along_x[k - 1]).start()

    loads[2].wait()
    loads[3].wait()
    tokens = chain_v.shape[0]
    chain_row = chain_v[...].astype(F32).reshape(1, tokens)
    chain_col[...] = jnp.transpose(jnp.broadcast_to(chain_row, (128, tokens))).reshape(chain_col.shape)
    mask_row = (pad_v[...].astype(F32).reshape(1, tokens) - 1.0) * 1000000000.0
    mask_col[...] = jnp.transpose(jnp.broadcast_to(mask_row, (128, tokens))).reshape(mask_col.shape)
    lane = lax.broadcasted_iota(jnp.int32, (rows, lanes), 1)
    query = lax.broadcasted_iota(jnp.int32, (rows, lanes), 0)
    pick = lane % rows == query
    own_chain = chain_col[t // CORES, core][:, 0:1]
    query_chain = jnp.sum(jnp.where(pick, own_chain, 0.0), axis=0, keepdims=True)
    loads[4].wait()
    gain = jnp.zeros((1, lanes), F32)
    lane_head = lax.broadcasted_iota(jnp.int32, (1, lanes), 1) // rows
    for h in range(heads):
        gain = jnp.where(lane_head == h, gain_s[h], gain)

    loads[5].wait()
    queries = dot(xbuf[own], wq[...]).astype(BF16)
    group_heads = heads // 2
    group_width = width // 2
    group_lanes = lanes // 2
    row_head = lax.broadcasted_iota(jnp.int32, (group_lanes, group_width), 0) // rows
    col_head = lax.broadcasted_iota(jnp.int32, (group_lanes, group_width), 1) // head_size
    for g in range(2):
        part = queries[:, g * group_width : (g + 1) * group_width]
        tiled = jnp.concatenate([part] * group_heads, axis=0)
        qexp[g] = jnp.where(row_head == col_head, tiled, jnp.zeros_like(tiled))

    loads[6].wait()
    loads[7].wait()
    wvt[...] = jnp.transpose(wv[...])

    def keys_values(at, count, first):
        block = xbuf[pl.ds(first, count // rows)].reshape(count, width)
        kbuf[at : at + count] = dot(block, wk[...]).astype(BF16)
        vbuf[:, at : at + count] = dot_t(wvt[...], block).astype(BF16)

    def scores(at, h, c):
        key = kbuf[at : at + quarter]
        found = jnp.concatenate(
            [dot_t(key[:, g * group_width : (g + 1) * group_width], qexp[g]) for g in range(2)], axis=1
        )
        bias = bbuf[pl.ds(h * QUAD, QUAD), pl.ds(c * (Y // CORES), Y // CORES)].reshape(quarter, lanes).astype(F32)
        key_chain = chain_col[pl.ds(h * X, X), c].reshape(quarter, 128)[:, 0:1]
        key_mask = mask_col[pl.ds(h * X, X), c].reshape(quarter, 128)[:, 0:1]
        found = found * (1.0 / math.sqrt(head_size)) + bias
        found = found + jnp.where(key_chain == query_chain, gain, 0.0)
        found = found + key_mask
        top = jnp.max(found, axis=0, keepdims=True)
        expo = jnp.exp(found - top)
        ebuf[at : at + quarter] = expo
        return top, jnp.sum(expo, axis=0, keepdims=True)

    sent = []
    for k in range(1, X):
        block = block_of(zh, other_x(k), core)
        recv_x(block)
        sent.append(send_x(block, X + k, sibling))

    @pl.when(place_z < QUAD - 1)
    def _():
        pl.semaphore_wait(ready_near, QUAD - 1 - place_z)

    for k in range(1, QUAD):

        @pl.when(place_z + k < QUAD)
        def _(k=k):
            z_copy(k, in_quad[k - 1]).start()

    @pl.when(late == 0)
    def _():
        pl.semaphore_wait(ready_cross, 1)
        z_copy(QUAD, opposite).start()

    z_copy(0, sibling, opposite_z).wait_recv()
    for k in range(1, QUAD):
        copy = z_copy(QUAD + k, in_quad[k - 1], opposite_z)
        copy.start()
        sent.append(copy)

    for k in range(X):
        recv_x(block_of(zh, other_x(k), 1 - core))
    keys_values(0, half, zh * per_half)

    for k in range(1, QUAD):
        z_copy(0, sibling, quad * QUAD + (place_z + k) % QUAD).wait_recv()

    @pl.when(y < Y - 1)
    def _():
        pl.semaphore_wait(ready_y, Y - 1 - y)

    sent += hand_on_y(0)

    far_block = block_of(1 - zh, cx, core)

    def far_copies():
        return [x_copy(far_block, 2 * X + n, who) for n, who in enumerate([sibling] + along_x_both)]

    def cross_step():
        for k in range(1, QUAD):
            z_copy(0, sibling, (1 - quad) * QUAD + (place_z + k) % QUAD).wait_recv()
        hand_on_y(1)

    def far_step():
        @pl.when(zh == 0)
        def _():
            pl.semaphore_wait(ready_far, 1)
            x_copy(own, 0, far).start()

        recv_x(far_block)
        for copy in far_copies():
            copy.start()

    @pl.when(late == 0)
    def _():
        cross_step()
        far_step()

    @pl.when(late == 1)
    def _():
        far_step()
        cross_step()

    for part in range(2):
        for k in range(1, Y):
            y_copy(0, part, sibling, (y + k) % Y).wait_recv()
    found = [scores(0, zh, 0), scores(quarter, zh, 1)]

    recv_x(block_of(1 - zh, cx, 1 - core))
    for k in range(1, X):
        for c in (core, 1 - core):
            recv_x(block_of(1 - zh, other_x(k), c))
    keys_values(half, half, (1 - zh) * per_half)
    found += [scores(half, 1 - zh, 0), scores(half + quarter, 1 - zh, 1)]

    top = functools.reduce(jnp.maximum, [f[0] for f in found])
    shares = [jnp.exp(f[0] - top) for f in found]
    total = sum(f[1] * share for f, share in zip(found, shares))
    for n, share in enumerate(shares):
        r = slice(n * quarter, (n + 1) * quarter)
        wbuf[r] = (ebuf[r] * (share / total)).astype(BF16)

    feature_head = lax.broadcasted_iota(jnp.int32, (group_width, group_lanes), 0) // head_size
    lane_of = lax.broadcasted_iota(jnp.int32, (group_width, group_lanes), 1) // rows
    place = pick[:, :group_lanes].astype(BF16)
    pieces = []
    for g in range(2):
        f = slice(g * group_width, (g + 1) * group_width)
        l = slice(g * group_lanes, (g + 1) * group_lanes)
        kept = jnp.where(feature_head == lane_of, dot(vbuf[f], wbuf[:, l]), 0.0).astype(BF16)
        pieces.append(dot_t(place, kept).astype(BF16))
    attended = jnp.concatenate(pieces, axis=1)

    loads[8].wait()
    projected = dot(attended, wo[...])
    ratio = jnp.full((1, width), step_s[0], jnp.int32).astype(F32) / (STEPS - 1)
    upper, lower = SIGMA_TOP ** (1.0 / RHO), SIGMA_LOW ** (1.0 / RHO)
    base = upper + ratio * (lower - upper)
    square = base * base
    sigma = SIGMA_DATA * (square * square * square * base)
    skip_scale = SIGMA_DATA**2 / (SIGMA_DATA**2 + sigma * sigma)
    out_scale = sigma / jnp.sqrt(sigma * sigma + SIGMA_DATA**2)
    out_ref[0] = (skip_scale * x_raw[0].astype(F32) + out_scale * projected).astype(BF16)

    for copy in sent + far_copies() + [y_copy(n, 1, sibling, y) for n in range(Y - 1)]:
        copy.wait_send()
    for n in range(X + 1):
        x_copy(own, n, far).wait_send()
    for n in range(1, QUAD + 1):
        z_copy(n, sibling).wait_send()


def shards(noisy, pair_bias, chain_ids, pad_mask, step_index, chain_gain, w_query, w_key, w_value, w_output):
    samples, rows, width = noisy.shape
    heads, _, keys_each = pair_bias.shape
    tokens = chain_ids.shape[0]
    blocks = tokens // rows
    lanes = heads * rows
    dma = pltpu.SemaphoreType.DMA
    weight = pltpu.VMEM((width, width), BF16)
    column = pltpu.VMEM((blocks // CORES, CORES, rows, 128), F32)
    large = [
        noisy, jnp.transpose(pair_bias, (0, 2, 1)), chain_ids, pad_mask, chain_gain,
        w_query, w_key, w_value, w_output,
    ]
    return pl.pallas_call(
        kernel,
        out_shape=jax.ShapeDtypeStruct((samples, rows, width), BF16),
        in_specs=[pl.BlockSpec(memory_space=pltpu.SMEM)] + [pl.BlockSpec(memory_space=pltpu.HBM)] * len(large),
        out_specs=pl.BlockSpec(memory_space=pltpu.VMEM),
        scratch_shapes=[
            pltpu.VMEM((samples, rows, width), BF16),
            pltpu.VMEM((heads, keys_each, rows), BF16),
            pltpu.VMEM((tokens,), jnp.int32),
            pltpu.VMEM((tokens,), jnp.int32),
            pltpu.SMEM((heads,), F32),
            weight, weight, weight, weight,
            pltpu.VMEM((blocks, rows, width), BF16),
            pltpu.VMEM((Z_LO, Y, keys_each, lanes), BF16),
            pltpu.VMEM((tokens, width), BF16),
            pltpu.VMEM((width, tokens), BF16),
            pltpu.VMEM((2, lanes // 2, width // 2), BF16),
            weight,
            pltpu.VMEM((tokens, lanes), F32),
            pltpu.VMEM((tokens, lanes), BF16),
            column, column,
            dma((len(large),)),
            dma((4 * X,)),
            dma((blocks,)),
            dma((Z_LO,)),
            dma((Z_LO,)),
            dma((2 * Y,)),
            dma((2 * Y,)),
            *[pltpu.SemaphoreType.REGULAR] * 6,
        ],
        compiler_params=pltpu.CompilerParams(
            collective_id=0, has_side_effects=True, vmem_limit_bytes=32 * 1024 * 1024
        ),
    )(step_index, *[pltpu.with_memory_space_constraint(a, pltpu.HBM) for a in large])


def solution(mesh):
    in_specs = (
        P("sample", "tok", None),
        P(None, "tok", "sample"),
        P(),
        P(),
        P("sample"),
        P(),
        P(),
        P(),
        P(),
        P(),
    )
    out_specs = P("sample", "tok", None)
    return jax.shard_map(shards, mesh=mesh, in_specs=in_specs, out_specs=out_specs, check_vma=False)
```

```python
import functools
import math

import jax
import jax.numpy as jnp
from jax import lax
from jax.experimental import pallas as pl
from jax.experimental.pallas import tpu as pltpu
from jax.sharding import PartitionSpec as P

STEPS = 200
SIGMA_DATA = 16.0
SIGMA_TOP = 160.0
SIGMA_LOW = 0.0004
RHO = 7

Y, Z_LO = 4, 8
X, CORES = 4, 2

MESH = pl.DeviceIdType.MESH
F32 = jnp.float32
BF16 = jnp.bfloat16
QUAD = Z_LO // 2


def layer_norm(values):
    xf = values.astype(F32)
    center = xf - jnp.mean(xf, axis=-1, keepdims=True)
    spread = jnp.mean(center * center, axis=-1, keepdims=True)
    return (center * lax.rsqrt(spread + 1e-05)).astype(BF16)


def dot(a, b):
    return lax.dot_general(a, b, (((1,), (0,)), ((), ())), preferred_element_type=F32)


def dot_t(a, b):
    return lax.dot_general(a, b, (((1,), (1,)), ((), ())), preferred_element_type=F32)


def kernel(
    step_s, x_hbm, bias_hbm, chain_hbm, pad_hbm, gain_hbm, wq_hbm, wk_hbm, wv_hbm, wo_hbm,
    out_ref,
    x_raw, far_raw, bias_raw, small, gain_s, weights,
    xbuf, bbuf, vbuf, qexp, wvt, ebuf, wbuf, chain_col, mask_col,
    lsem, xs, xr, bzs, bzr, bys, byr, ready,
):
    heads, keys_each, rows = bias_hbm.shape
    width = x_hbm.shape[2]
    per_half = xbuf.shape[0] // 2
    half = per_half * rows
    quarter = half // CORES
    head_size = width // heads
    lanes = heads * rows

    s, t = lax.axis_index("sample"), lax.axis_index("tok")
    y, zl = s % Y, s // Y
    core, cx, zh = t % CORES, (t // CORES) % X, t // (CORES * X)
    quad, place_z = zl // QUAD, zl % QUAD
    late = (quad + zh * (place_z // 2)) % 2
    ready_x, ready_core, ready_y, ready_near, ready_cross, ready_far = (ready.at[n] for n in range(6))

    def tok_of(h, x, c):
        return h * (X * CORES) + x * CORES + c

    def block_of(h, x, c):
        return h * per_half + c * X + x

    def other_x(k):
        return (cx + k) % X

    far = (s, tok_of(1 - zh, cx, core))
    sibling = (s, tok_of(zh, cx, 1 - core))
    along_x = [(s, tok_of(zh, other_x(k), core)) for k in range(1, X)]
    along_y = [(zl * Y + (y + k) % Y, t) for k in range(1, Y)]
    in_quad = [((quad * QUAD + (place_z + k) % QUAD) * Y + y, t) for k in range(1, QUAD)]
    opposite_z = (1 - quad) * QUAD + place_z
    opposite = (opposite_z * Y + y, t)

    def signal(semaphore, who):
        pl.semaphore_signal(semaphore, inc=1, device_id=who, device_id_type=MESH)

    barrier = pltpu.get_barrier_semaphore()

    @pl.when(zh == 0)
    def _():
        signal(barrier, far)

    @pl.when(core == CORES - 1)
    def _():
        signal(barrier, sibling)

    for k in range(1, X):

        @pl.when(cx + k < X)
        def _(k=k):
            signal(barrier, along_x[k - 1])

    for k in range(1, Y):

        @pl.when(y + k < Y)
        def _(k=k):
            signal(barrier, along_y[k - 1])

    for k in range(1, QUAD):

        @pl.when(place_z + k < QUAD)
        def _(k=k):
            signal(barrier, in_quad[k - 1])

    @pl.when(late == 0)
    def _():
        signal(barrier, opposite)

    loads = [
        (x_hbm, x_raw, 0), (bias_hbm, bias_raw, 1), (chain_hbm, small.at[0], 2), (pad_hbm, small.at[1], 2),
        (gain_hbm, gain_s, 3), (wq_hbm, weights.at[0], 4), (wk_hbm, weights.at[1], 5), (wv_hbm, weights.at[2], 5),
        (wo_hbm, weights.at[3], 6),
    ]
    for src, dst, n in loads:
        pltpu.make_async_copy(src, dst, lsem.at[n]).start()

    def loaded(ref, n):
        pltpu.make_async_copy(ref, ref, lsem.at[n]).wait()

    def remote(ref, send, recv, who):
        return pltpu.make_async_remote_copy(
            src_ref=ref, dst_ref=ref, send_sem=send, recv_sem=recv, device_id=who, device_id_type=MESH
        )

    FAR = X

    def send_x(block, n, who):
        remote(xbuf.at[block], xs, xr.at[n], who).start()

    def recv_x(blocks, n):
        remote(blocks, xs, xr.at[n], sibling).wait_recv()

    def send_z(n, who, there):
        remote(bbuf.at[there, y], bzs, bzr.at[n], who).start()

    def recv_z(blocks, n):
        remote(blocks, bzs, bzr.at[n], sibling).wait_recv()

    def hand_on_y(part):
        q = (quad + part) % 2
        for who in along_y:
            remote(bbuf.at[pl.ds(q * QUAD, QUAD), y], bys, byr, who).start()

    def send_far():
        pltpu.make_async_remote_copy(
            src_ref=x_hbm, dst_ref=far_raw, send_sem=xs, recv_sem=xr.at[FAR], device_id=far, device_id_type=MESH
        ).start()

    earlier = zh + (CORES - 1 - core) + cx + y + place_z + late

    @pl.when(earlier > 0)
    def _():
        pl.semaphore_wait(barrier, earlier)

    @pl.when(zh == 1)
    def _():
        signal(ready_far, far)
        send_far()

    own = block_of(zh, cx, core)
    loaded(x_raw, 0)
    xbuf[own] = layer_norm(x_raw[0])

    loaded(bias_raw, 1)
    bbuf[zl, y] = jnp.concatenate([bias_raw[h] for h in range(heads)], axis=1)

    for k in range(1, X):

        @pl.when(cx + k >= X)
        def _(k=k):
            signal(ready_x, along_x[k - 1])
            send_x(own, X - k, along_x[k - 1])

    @pl.when(core == 0)
    def _():
        signal(ready_core, sibling)
        send_x(own, 0, sibling)

    for k in range(1, Y):

        @pl.when(y + k >= Y)
        def _(k=k):
            signal(ready_y, along_y[k - 1])

    for k in range(1, QUAD):

        @pl.when(place_z + k >= QUAD)
        def _(k=k):
            signal(ready_near, in_quad[k - 1])
            send_z(0, in_quad[k - 1], zl)

    @pl.when(late == 1)
    def _():
        signal(ready_cross, opposite)
        send_z(1, opposite, zl)

    @pl.when(cx < X - 1)
    def _():
        pl.semaphore_wait(ready_x, X - 1 - cx)

    for k in range(1, X):

        @pl.when(cx + k < X)
        def _(k=k):
            send_x(own, X - k, along_x[k - 1])

    @pl.when(place_z < QUAD - 1)
    def _():
        pl.semaphore_wait(ready_near, QUAD - 1 - place_z)

    for k in range(1, QUAD):

        @pl.when(place_z + k < QUAD)
        def _(k=k):
            send_z(0, in_quad[k - 1], zl)

    @pl.when(late == 0)
    def _():
        pl.semaphore_wait(ready_cross, 1)
        send_z(1, opposite, zl)

    @pl.when(core == CORES - 1)
    def _():
        pl.semaphore_wait(ready_core, 1)
        send_x(own, 0, sibling)

    loaded(small, 2)
    tokens = small.shape[1]
    chain_row = small[0:1].astype(F32)
    chain_col[...] = jnp.transpose(jnp.broadcast_to(chain_row, (128, tokens))).reshape(chain_col.shape)
    mask_row = (small[1:2].astype(F32) - 1.0) * 1000000000.0
    mask_col[...] = jnp.transpose(jnp.broadcast_to(mask_row, (128, tokens))).reshape(mask_col.shape)
    lane = lax.broadcasted_iota(jnp.int32, (rows, lanes), 1)
    query = lax.broadcasted_iota(jnp.int32, (rows, lanes), 0)
    pick = lane % rows == query
    own_chain = chain_col[t // CORES, core][:, 0:1]
    query_chain = jnp.sum(jnp.where(pick, own_chain, 0.0), axis=0, keepdims=True)
    loaded(gain_s, 3)
    gain = jnp.zeros((1, lanes), F32)
    lane_head = lax.broadcasted_iota(jnp.int32, (1, lanes), 1) // rows
    for h in range(heads):
        gain = jnp.where(lane_head == h, gain_s[h], gain)

    loaded(weights.at[0], 4)
    queries = dot(xbuf[own], weights[0]).astype(BF16)
    group_heads = heads // 2
    group_width = width // 2
    group_lanes = lanes // 2
    row_head = lax.broadcasted_iota(jnp.int32, (group_lanes, group_width), 0) // rows
    col_head = lax.broadcasted_iota(jnp.int32, (group_lanes, group_width), 1) // head_size
    for g in range(2):
        part = queries[:, g * group_width : (g + 1) * group_width]
        tiled = jnp.concatenate([part] * group_heads, axis=0)
        qexp[g] = jnp.where(row_head == col_head, tiled, jnp.zeros_like(tiled))

    loaded(weights.at[pl.ds(1, 2)], 5)
    wvt[...] = jnp.transpose(weights[2])

    def values(h):
        block = xbuf[pl.ds(h * per_half, per_half)].reshape(half, width)
        return dot_t(wvt[...], block).astype(BF16)

    def raw_scores(h, c):
        block = xbuf[pl.ds(block_of(h, 0, c), X)].reshape(quarter, width)
        key = dot(block, weights[1]).astype(BF16)
        return jnp.concatenate(
            [dot_t(key[:, g * group_width : (g + 1) * group_width], qexp[g]) for g in range(2)], axis=1
        )

    def scores(found, at, h, c):
        bias = bbuf[pl.ds(h * QUAD, QUAD), pl.ds(c * (Y // CORES), Y // CORES)].reshape(quarter, lanes).astype(F32)
        key_chain = chain_col[pl.ds(h * X, X), c].reshape(quarter, 128)[:, 0:1]
        key_mask = mask_col[pl.ds(h * X, X), c].reshape(quarter, 128)[:, 0:1]
        found = found * (1.0 / math.sqrt(head_size)) + bias
        found = found + jnp.where(key_chain == query_chain, gain, 0.0)
        found = found + key_mask
        top = jnp.max(found, axis=0, keepdims=True)
        expo = jnp.exp(found - top)
        ebuf[at] = expo
        return at, top, jnp.sum(expo, axis=0, keepdims=True)

    def part_of(c):
        return pl.ds(pl.multiple_of(half + c * quarter, quarter), quarter)

    for k in range(1, X):
        block = block_of(zh, other_x(k), core)
        recv_x(xbuf.at[block], k)
        send_x(block, 0, sibling)

    recv_z(bbuf.at[opposite_z, y], 1)
    for who in in_quad:
        send_z(2, who, opposite_z)

    recv_z(bbuf.at[pl.ds(0, QUAD - 1), y], 0)

    @pl.when(y < Y - 1)
    def _():
        pl.semaphore_wait(ready_y, Y - 1 - y)

    hand_on_y(0)

    @pl.when(zh == 0)
    def _():
        pl.semaphore_wait(ready_far, 1)
        send_far()

    recv_x(xbuf.at[pl.ds(0, X)], 0)
    vbuf[:, 0:half] = values(zh)
    for c in range(CORES):
        ebuf[c * quarter : (c + 1) * quarter] = raw_scores(zh, c)

    far_block = block_of(1 - zh, cx, core)

    def cross_step():
        recv_z(bbuf.at[pl.ds(0, QUAD - 1), y], 2)
        hand_on_y(1)

    def far_step():
        recv_x(far_raw, FAR)
        xbuf[far_block] = layer_norm(far_raw[0])
        for k in (2, 1, 3):
            send_x(far_block, FAR + X - k, along_x[k - 1])
        send_x(far_block, 2 * X, sibling)

    @pl.when(late == 0)
    def _():
        cross_step()
        far_step()

    @pl.when(late == 1)
    def _():
        far_step()
        cross_step()

    for k in (1, 3, 2):
        block = block_of(1 - zh, other_x(k), core)
        recv_x(xbuf.at[block], FAR + k)
        send_x(block, 2 * X, sibling)

    remote(bbuf.at[pl.ds(0, 2 * (Y - 1))], bys, byr, sibling).wait_recv()
    found = []
    for c in range(CORES):
        at = pl.ds(c * quarter, quarter)
        found.append(scores(ebuf[at], at, zh, c))
    found.append(scores(raw_scores(1 - zh, core), part_of(core), 1 - zh, core))
    recv_x(xbuf.at[pl.ds(0, X)], 2 * X)
    found.append(scores(raw_scores(1 - zh, 1 - core), part_of(1 - core), 1 - zh, 1 - core))
    vbuf[:, half:] = values(1 - zh)

    top = functools.reduce(jnp.maximum, [f[1] for f in found])
    shares = [jnp.exp(f[1] - top) for f in found]
    total = sum(f[2] * share for f, share in zip(found, shares))
    for (at, _, _), share in zip(found, shares):
        wbuf[at] = (ebuf[at] * (share / total)).astype(BF16)

    feature_head = lax.broadcasted_iota(jnp.int32, (group_width, group_lanes), 0) // head_size
    lane_of = lax.broadcasted_iota(jnp.int32, (group_width, group_lanes), 1) // rows
    place = pick[:, :group_lanes].astype(BF16)
    pieces = []
    for g in range(2):
        f = slice(g * group_width, (g + 1) * group_width)
        l = slice(g * group_lanes, (g + 1) * group_lanes)
        kept = jnp.where(feature_head == lane_of, dot(vbuf[f], wbuf[:, l]), 0.0).astype(BF16)
        pieces.append(dot_t(place, kept).astype(BF16))
    attended = jnp.concatenate(pieces, axis=1)

    loaded(weights.at[3], 6)
    projected = dot(attended, weights[3])
    ratio = jnp.full((1, width), step_s[0], jnp.int32).astype(F32) / (STEPS - 1)
    upper, lower = SIGMA_TOP ** (1.0 / RHO), SIGMA_LOW ** (1.0 / RHO)
    base = upper + ratio * (lower - upper)
    square = base * base
    sigma = SIGMA_DATA * (square * square * square * base)
    skip_scale = SIGMA_DATA**2 / (SIGMA_DATA**2 + sigma * sigma)
    out_scale = sigma / jnp.sqrt(sigma * sigma + SIGMA_DATA**2)
    out_ref[0] = (skip_scale * x_raw[0].astype(F32) + out_scale * projected).astype(BF16)

    remote(xbuf.at[pl.ds(0, 4 * X - 1)], xs, xr.at[0], sibling).wait_send()
    remote(bbuf.at[pl.ds(0, 2 * QUAD - 1), y], bzs, bzr.at[0], sibling).wait_send()
    remote(bbuf.at[pl.ds(0, 2 * (Y - 1))], bys, byr, sibling).wait_send()


def shards(noisy, pair_bias, chain_ids, pad_mask, step_index, chain_gain, w_query, w_key, w_value, w_output):
    samples, rows, width = noisy.shape
    heads, _, keys_each = pair_bias.shape
    tokens = chain_ids.shape[0]
    blocks = tokens // rows
    lanes = heads * rows
    dma = pltpu.SemaphoreType.DMA
    column = pltpu.VMEM((blocks // CORES, CORES, rows, 128), F32)
    large = [
        noisy, jnp.transpose(pair_bias, (0, 2, 1)), chain_ids, pad_mask, chain_gain,
        w_query, w_key, w_value, w_output,
    ]
    return pl.pallas_call(
        kernel,
        out_shape=jax.ShapeDtypeStruct((samples, rows, width), BF16),
        in_specs=[pl.BlockSpec(memory_space=pltpu.SMEM)] + [pl.BlockSpec(memory_space=pltpu.HBM)] * len(large),
        out_specs=pl.BlockSpec(memory_space=pltpu.VMEM),
        scratch_shapes=[
            pltpu.VMEM((samples, rows, width), BF16),
            pltpu.VMEM((samples, rows, width), BF16),
            pltpu.VMEM((heads, keys_each, rows), BF16),
            pltpu.VMEM((2, tokens), jnp.int32),
            pltpu.SMEM((heads,), F32),
            pltpu.VMEM((4, width, width), BF16),
            pltpu.VMEM((blocks, rows, width), BF16),
            pltpu.VMEM((Z_LO, Y, keys_each, lanes), BF16),
            pltpu.VMEM((width, tokens), BF16),
            pltpu.VMEM((2, lanes // 2, width // 2), BF16),
            pltpu.VMEM((width, width), BF16),
            pltpu.VMEM((tokens, lanes), F32),
            pltpu.VMEM((tokens, lanes), BF16),
            column, column,
            dma((7,)),
            dma,
            dma((2 * X + 1,)),
            dma,
            dma((3,)),
            dma,
            dma,
            pltpu.SemaphoreType.REGULAR((6,)),
        ],
        compiler_params=pltpu.CompilerParams(
            collective_id=0, has_side_effects=True, vmem_limit_bytes=32 * 1024 * 1024
        ),
    )(step_index, *[pltpu.with_memory_space_constraint(a, pltpu.HBM) for a in large])


def solution(mesh):
    in_specs = (
        P("sample", "tok", None),
        P(None, "tok", "sample"),
        P(),
        P(),
        P("sample"),
        P(),
        P(),
        P(),
        P(),
        P(),
    )
    out_specs = P("sample", "tok", None)
    return jax.shard_map(shards, mesh=mesh, in_specs=in_specs, out_specs=out_specs, check_vma=False)
```

```python
import functools
import math

import jax
import jax.numpy as jnp
from jax import lax
from jax.experimental import pallas as pl
from jax.experimental.pallas import tpu as pltpu
from jax.sharding import PartitionSpec as P

STEPS = 200
SIGMA_DATA = 16.0
SIGMA_TOP = 160.0
SIGMA_LOW = 0.0004
RHO = 7

Y, Z_LO = 4, 8
X, CORES = 4, 2

MESH = pl.DeviceIdType.MESH
F32 = jnp.float32
BF16 = jnp.bfloat16
QUAD = Z_LO // 2


def layer_norm(values):
    xf = values.astype(F32)
    center = xf - jnp.mean(xf, axis=-1, keepdims=True)
    spread = jnp.mean(center * center, axis=-1, keepdims=True)
    return (center * lax.rsqrt(spread + 1e-05)).astype(BF16)


def dot(a, b):
    return lax.dot_general(a, b, (((1,), (0,)), ((), ())), preferred_element_type=F32)


def dot_t(a, b):
    return lax.dot_general(a, b, (((1,), (1,)), ((), ())), preferred_element_type=F32)


def kernel(
    step_s, x_hbm, bias_hbm, chain_hbm, pad_hbm, gain_hbm, wq_hbm, wk_hbm, wv_hbm, wo_hbm,
    out_ref,
    x_raw, far_raw, bias_raw, small, gain_s, weights,
    xbuf, bbuf, vbuf, qexp, ebuf, wbuf, chain_col, mask_col,
    lsem, xs, xr, bzs, bzr, bys, byr, ready,
):
    heads, keys_each, rows = bias_hbm.shape
    width = x_hbm.shape[2]
    per_half = xbuf.shape[0] // 2
    half = per_half * rows
    quarter = half // CORES
    head_size = width // heads
    lanes = heads * rows

    s, t = lax.axis_index("sample"), lax.axis_index("tok")
    y, zl = s % Y, s // Y
    core, cx, zh = t % CORES, (t // CORES) % X, t // (CORES * X)
    quad, place_z = zl // QUAD, zl % QUAD
    late = (quad + zh * (place_z // 2)) % 2
    ready_x, ready_core, ready_y, ready_near, ready_cross, ready_far = (ready.at[n] for n in range(6))

    def tok_of(h, x, c):
        return h * (X * CORES) + x * CORES + c

    def block_of(h, x, c):
        return h * per_half + c * X + x

    def other_x(k):
        return (cx + k) % X

    far = (s, tok_of(1 - zh, cx, core))
    sibling = (s, tok_of(zh, cx, 1 - core))
    along_x = [(s, tok_of(zh, other_x(k), core)) for k in range(1, X)]
    along_y = [(zl * Y + (y + k) % Y, t) for k in range(1, Y)]
    in_quad = [((quad * QUAD + (place_z + k) % QUAD) * Y + y, t) for k in range(1, QUAD)]
    opposite_z = (1 - quad) * QUAD + place_z
    opposite = (opposite_z * Y + y, t)

    def signal(semaphore, who):
        pl.semaphore_signal(semaphore, inc=1, device_id=who, device_id_type=MESH)

    barrier = pltpu.get_barrier_semaphore()

    @pl.when(zh == 0)
    def _():
        signal(barrier, far)

    @pl.when(core == CORES - 1)
    def _():
        signal(barrier, sibling)

    for k in range(1, X):

        @pl.when(cx + k < X)
        def _(k=k):
            signal(barrier, along_x[k - 1])

    for k in range(1, Y):

        @pl.when(y + k < Y)
        def _(k=k):
            signal(barrier, along_y[k - 1])

    for k in range(1, QUAD):

        @pl.when(place_z + k < QUAD)
        def _(k=k):
            signal(barrier, in_quad[k - 1])

    @pl.when(late == 0)
    def _():
        signal(barrier, opposite)

    loads = [
        (x_hbm, x_raw, 0), (bias_hbm, bias_raw, 1), (chain_hbm, small.at[0], 2), (pad_hbm, small.at[1], 2),
        (gain_hbm, gain_s, 3), (wq_hbm, weights.at[0], 4), (wk_hbm, weights.at[1], 5), (wv_hbm, weights.at[2], 5),
        (wo_hbm, weights.at[3], 6),
    ]
    for src, dst, n in loads:
        pltpu.make_async_copy(src, dst, lsem.at[n]).start()

    def loaded(ref, n):
        pltpu.make_async_copy(ref, ref, lsem.at[n]).wait()

    def remote(ref, send, recv, who):
        return pltpu.make_async_remote_copy(
            src_ref=ref, dst_ref=ref, send_sem=send, recv_sem=recv, device_id=who, device_id_type=MESH
        )

    FAR = X

    def send_x(block, n, who, piece=slice(None)):
        remote(xbuf.at[block, piece], xs, xr.at[n], who).start()

    def recv_x(blocks, n):
        remote(blocks, xs, xr.at[n], sibling).wait_recv()

    def send_z(n, who, there):
        remote(bbuf.at[there, y], bzs, bzr.at[n], who).start()

    def recv_z(blocks, n):
        remote(blocks, bzs, bzr.at[n], sibling).wait_recv()

    def hand_on_y(blocks):
        for who in along_y:
            remote(blocks, bys, byr, who).start()

    PIECES = 2
    pieces = [pl.ds(p * (rows // PIECES), rows // PIECES) for p in range(PIECES)]

    def send_far():
        for p, piece in enumerate(pieces):
            pltpu.make_async_remote_copy(
                src_ref=x_raw.at[0, piece], dst_ref=far_raw.at[0, piece], send_sem=xs, recv_sem=xr.at[FAR + X * p],
                device_id=far, device_id_type=MESH,
            ).start()

    earlier = zh + (CORES - 1 - core) + cx + y + place_z + late

    @pl.when(earlier > 0)
    def _():
        pl.semaphore_wait(barrier, earlier)

    loaded(x_raw, 0)

    @pl.when(zh == 1)
    def _():
        signal(ready_far, far)
        send_far()

    own = block_of(zh, cx, core)

    loaded(bias_raw, 1)
    bbuf[zl, y] = jnp.concatenate([bias_raw[h] for h in range(heads)], axis=1)

    for k in range(1, Y):

        @pl.when(y + k >= Y)
        def _(k=k):
            signal(ready_y, along_y[k - 1])

    for k in range(1, QUAD):

        @pl.when(place_z + k >= QUAD)
        def _(k=k):
            signal(ready_near, in_quad[k - 1])
            send_z(0, in_quad[k - 1], zl)

    @pl.when(late == 1)
    def _():
        signal(ready_cross, opposite)
        send_z(1, opposite, zl)

    xbuf[own] = layer_norm(x_raw[0])


    for k in range(1, X):

        @pl.when(cx + k >= X)
        def _(k=k):
            signal(ready_x, along_x[k - 1])
            send_x(own, X - k, along_x[k - 1])

    @pl.when(core == 0)
    def _():
        signal(ready_core, sibling)
        send_x(own, 0, sibling)

    @pl.when(cx < X - 1)
    def _():
        pl.semaphore_wait(ready_x, X - 1 - cx)

    for k in range(1, X):

        @pl.when(cx + k < X)
        def _(k=k):
            send_x(own, X - k, along_x[k - 1])

    @pl.when(place_z < QUAD - 1)
    def _():
        pl.semaphore_wait(ready_near, QUAD - 1 - place_z)

    for k in range(1, QUAD):

        @pl.when(place_z + k < QUAD)
        def _(k=k):
            send_z(0, in_quad[k - 1], zl)

    @pl.when(late == 0)
    def _():
        pl.semaphore_wait(ready_cross, 1)
        send_z(1, opposite, zl)

    @pl.when(core == CORES - 1)
    def _():
        pl.semaphore_wait(ready_core, 1)
        send_x(own, 0, sibling)

    loaded(small, 2)
    tokens = small.shape[1]
    chain_row = small[0:1].astype(F32)
    chain_col[...] = jnp.transpose(jnp.broadcast_to(chain_row, (128, tokens))).reshape(chain_col.shape)
    mask_row = (small[1:2].astype(F32) - 1.0) * 1000000000.0
    mask_col[...] = jnp.transpose(jnp.broadcast_to(mask_row, (128, tokens))).reshape(mask_col.shape)
    lane = lax.broadcasted_iota(jnp.int32, (rows, lanes), 1)
    query = lax.broadcasted_iota(jnp.int32, (rows, lanes), 0)
    pick = lane % rows == query
    own_chain = chain_col[t // CORES, core][:, 0:1]
    query_chain = jnp.sum(jnp.where(pick, own_chain, 0.0), axis=0, keepdims=True)
    loaded(gain_s, 3)
    gain = jnp.zeros((1, lanes), F32)
    lane_head = lax.broadcasted_iota(jnp.int32, (1, lanes), 1) // rows
    for h in range(heads):
        gain = jnp.where(lane_head == h, gain_s[h], gain)

    loaded(weights.at[0], 4)
    queries = dot(xbuf[own], weights[0]).astype(BF16)
    group_heads = heads // 2
    group_width = width // 2
    group_lanes = lanes // 2
    row_head = lax.broadcasted_iota(jnp.int32, (group_lanes, group_width), 0) // rows
    col_head = lax.broadcasted_iota(jnp.int32, (group_lanes, group_width), 1) // head_size
    for g in range(2):
        part = queries[:, g * group_width : (g + 1) * group_width]
        tiled = jnp.concatenate([part] * group_heads, axis=0)
        qexp[g] = jnp.where(row_head == col_head, tiled, jnp.zeros_like(tiled))

    loaded(weights.at[pl.ds(1, 2)], 5)

    def values(first, count):
        block = xbuf[pl.ds(first, count // rows)].reshape(count, width)
        return jnp.transpose(dot(block, weights[2]).astype(BF16))

    def raw_scores(h, c):
        block = xbuf[pl.ds(block_of(h, 0, c), X)].reshape(quarter, width)
        key = dot(block, weights[1]).astype(BF16)
        return jnp.concatenate(
            [dot_t(key[:, g * group_width : (g + 1) * group_width], qexp[g]) for g in range(2)], axis=1
        )

    def scores(found, at, h, c):
        bias = bbuf[pl.ds(h * QUAD, QUAD), pl.ds(c * (Y // CORES), Y // CORES)].reshape(quarter, lanes).astype(F32)
        key_chain = chain_col[pl.ds(h * X, X), c].reshape(quarter, 128)[:, 0:1]
        key_mask = mask_col[pl.ds(h * X, X), c].reshape(quarter, 128)[:, 0:1]
        found = found * (1.0 / math.sqrt(head_size)) + bias
        found = found + jnp.where(key_chain == query_chain, gain, 0.0)
        found = found + key_mask
        top = jnp.max(found, axis=0, keepdims=True)
        expo = jnp.exp(found - top)
        ebuf[at] = expo
        return at, top, jnp.sum(expo, axis=0, keepdims=True)

    def part_of(c):
        return pl.ds(pl.multiple_of(half + c * quarter, quarter), quarter)

    for k in range(1, X):
        block = block_of(zh, other_x(k), core)
        recv_x(xbuf.at[block], k)
        send_x(block, 0, sibling)

    recv_z(bbuf.at[opposite_z, y], 1)
    for k in range(1, QUAD):
        send_z(1 + QUAD - k, in_quad[k - 1], opposite_z)

    @pl.when(y < Y - 1)
    def _():
        pl.semaphore_wait(ready_y, Y - 1 - y)

    hand_on_y(bbuf.at[opposite_z, y])

    recv_z(bbuf.at[pl.ds(0, QUAD - 1), y], 0)

    hand_on_y(bbuf.at[pl.ds(quad * QUAD, QUAD), y])

    @pl.when((zh == 0) & (zl > 0))
    def _():
        pl.semaphore_wait(ready_far, 1)
        send_far()

    recv_x(xbuf.at[pl.ds(0, X)], 0)
    vbuf[:, 0:half] = values(zh * per_half, half)
    for c in range(CORES):
        ebuf[c * quarter : (c + 1) * quarter] = raw_scores(zh, c)

    far_block = block_of(1 - zh, cx, core)

    def cross_step():
        for k in range(1, QUAD):
            there = (1 - quad) * QUAD + (place_z + k) % QUAD
            recv_z(bbuf.at[there, y], 1 + k)
            hand_on_y(bbuf.at[there, y])

    def far_step():
        for p, piece in enumerate(pieces):
            recv_x(far_raw.at[0, piece], FAR + X * p)
            xbuf[far_block, piece] = layer_norm(far_raw[0, piece])
            for k in (2, 1, 3):
                send_x(far_block, FAR + X * p + X - k, along_x[k - 1], piece)
            send_x(far_block, FAR + X * PIECES, sibling, piece)

    @pl.when(late == 0)
    def _():
        cross_step()
        far_step()

        @pl.when((zh == 0) & (zl == 0))
        def _():
            pl.semaphore_wait(ready_far, 1)
            send_far()

    @pl.when(late == 1)
    def _():
        far_step()
        cross_step()

    for p, piece in enumerate(pieces):
        for k in (1, 3, 2):
            block = block_of(1 - zh, other_x(k), core)
            recv_x(xbuf.at[block, piece], FAR + X * p + k)
            send_x(block, FAR + X * PIECES, sibling, piece)

    remote(bbuf.at[pl.ds(0, 2 * (Y - 1))], bys, byr, sibling).wait_recv()
    found = []
    for c in range(CORES):
        at = pl.ds(c * quarter, quarter)
        found.append(scores(ebuf[at], at, zh, c))
    found.append(scores(raw_scores(1 - zh, core), part_of(core), 1 - zh, core))
    vbuf[:, part_of(core)] = values(block_of(1 - zh, 0, core), quarter)
    recv_x(xbuf.at[pl.ds(0, X)], FAR + X * PIECES)
    found.append(scores(raw_scores(1 - zh, 1 - core), part_of(1 - core), 1 - zh, 1 - core))
    vbuf[:, part_of(1 - core)] = values(block_of(1 - zh, 0, 1 - core), quarter)

    top = functools.reduce(jnp.maximum, [f[1] for f in found])
    shares = [jnp.exp(f[1] - top) for f in found]
    total = sum(f[2] * share for f, share in zip(found, shares))
    for (at, _, _), share in zip(found, shares):
        wbuf[at] = (ebuf[at] * (share / total)).astype(BF16)

    feature_head = lax.broadcasted_iota(jnp.int32, (group_width, group_lanes), 0) // head_size
    lane_of = lax.broadcasted_iota(jnp.int32, (group_width, group_lanes), 1) // rows
    place = pick[:, :group_lanes].astype(BF16)
    kept = []
    for g in range(2):
        f = slice(g * group_width, (g + 1) * group_width)
        l = slice(g * group_lanes, (g + 1) * group_lanes)
        kept.append(jnp.where(feature_head == lane_of, dot(vbuf[f], wbuf[:, l]), 0.0).astype(BF16))
    attended = dot_t(place, jnp.concatenate(kept, axis=0)).astype(BF16)

    loaded(weights.at[3], 6)
    projected = dot(attended, weights[3])
    ratio = jnp.full((1, width), step_s[0], jnp.int32).astype(F32) / (STEPS - 1)
    upper, lower = SIGMA_TOP ** (1.0 / RHO), SIGMA_LOW ** (1.0 / RHO)
    base = upper + ratio * (lower - upper)
    square = base * base
    sigma = SIGMA_DATA * (square * square * square * base)
    skip_scale = SIGMA_DATA**2 / (SIGMA_DATA**2 + sigma * sigma)
    out_scale = sigma / jnp.sqrt(sigma * sigma + SIGMA_DATA**2)
    out_ref[0] = (skip_scale * x_raw[0].astype(F32) + out_scale * projected).astype(BF16)

    remote(xbuf.at[pl.ds(0, 4 * X - 1)], xs, xr.at[0], sibling).wait_send()
    remote(bbuf.at[pl.ds(0, 2 * QUAD - 1), y], bzs, bzr.at[0], sibling).wait_send()
    remote(bbuf.at[pl.ds(0, 2 * (Y - 1))], bys, byr, sibling).wait_send()


def shards(noisy, pair_bias, chain_ids, pad_mask, step_index, chain_gain, w_query, w_key, w_value, w_output):
    samples, rows, width = noisy.shape
    heads, _, keys_each = pair_bias.shape
    tokens = chain_ids.shape[0]
    blocks = tokens // rows
    lanes = heads * rows
    dma = pltpu.SemaphoreType.DMA
    column = pltpu.VMEM((blocks // CORES, CORES, rows, 128), F32)
    large = [
        noisy, jnp.transpose(pair_bias, (0, 2, 1)), chain_ids, pad_mask, chain_gain,
        w_query, w_key, w_value, w_output,
    ]
    return pl.pallas_call(
        kernel,
        out_shape=jax.ShapeDtypeStruct((samples, rows, width), BF16),
        in_specs=[pl.BlockSpec(memory_space=pltpu.SMEM)] + [pl.BlockSpec(memory_space=pltpu.HBM)] * len(large),
        out_specs=pl.BlockSpec(memory_space=pltpu.VMEM),
        scratch_shapes=[
            pltpu.VMEM((samples, rows, width), BF16),
            pltpu.VMEM((samples, rows, width), BF16),
            pltpu.VMEM((heads, keys_each, rows), BF16),
            pltpu.VMEM((2, tokens), jnp.int32),
            pltpu.SMEM((heads,), F32),
            pltpu.VMEM((4, width, width), BF16),
            pltpu.VMEM((blocks, rows, width), BF16),
            pltpu.VMEM((Z_LO, Y, keys_each, lanes), BF16),
            pltpu.VMEM((width, tokens), BF16),
            pltpu.VMEM((2, lanes // 2, width // 2), BF16),
            pltpu.VMEM((tokens, lanes), F32),
            pltpu.VMEM((tokens, lanes), BF16),
            column, column,
            dma((7,)),
            dma,
            dma((3 * X + 1,)),
            dma,
            dma((1 + QUAD,)),
            dma,
            dma,
            pltpu.SemaphoreType.REGULAR((6,)),
        ],
        compiler_params=pltpu.CompilerParams(
            collective_id=0, has_side_effects=True, vmem_limit_bytes=32 * 1024 * 1024
        ),
    )(step_index, *[pltpu.with_memory_space_constraint(a, pltpu.HBM) for a in large])


def solution(mesh):
    in_specs = (
        P("sample", "tok", None),
        P(None, "tok", "sample"),
        P(),
        P(),
        P("sample"),
        P(),
        P(),
        P(),
        P(),
        P(),
    )
    out_specs = P("sample", "tok", None)
    return jax.shard_map(shards, mesh=mesh, in_specs=in_specs, out_specs=out_specs, check_vma=False)
```

```python
import functools
import math

import jax
import jax.numpy as jnp
from jax import lax
from jax.experimental import pallas as pl
from jax.experimental.pallas import tpu as pltpu
from jax.sharding import PartitionSpec as P

STEPS = 200
SIGMA_DATA = 16.0
SIGMA_TOP = 160.0
SIGMA_LOW = 0.0004
RHO = 7

Y, Z_LO = 4, 8
X, CORES = 4, 2

MESH = pl.DeviceIdType.MESH
F32 = jnp.float32
BF16 = jnp.bfloat16
QUAD = Z_LO // 2


def layer_norm(values):
    xf = values.astype(F32)
    center = xf - jnp.mean(xf, axis=-1, keepdims=True)
    spread = jnp.mean(center * center, axis=-1, keepdims=True)
    return (center * lax.rsqrt(spread + 1e-05)).astype(BF16)


def dot(a, b):
    return lax.dot_general(a, b, (((1,), (0,)), ((), ())), preferred_element_type=F32)


def dot_t(a, b):
    return lax.dot_general(a, b, (((1,), (1,)), ((), ())), preferred_element_type=F32)


def kernel(
    step_s, x_hbm, bias_hbm, chain_hbm, pad_hbm, gain_hbm, wq_hbm, wk_hbm, wv_hbm, wo_hbm,
    out_ref,
    x_raw, far_raw, bias_raw, small, gain_s, weights,
    xbuf, bbuf, vbuf, qexp, ebuf, wbuf, chain_col, mask_col,
    lsem, xs, xr, bzs, bzr, bys, byr, ready,
):
    heads, keys_each, rows = bias_hbm.shape
    width = x_hbm.shape[2]
    per_half = xbuf.shape[0] // 2
    half = per_half * rows
    quarter = half // CORES
    head_size = width // heads
    lanes = heads * rows

    s, t = lax.axis_index("sample"), lax.axis_index("tok")
    y, zl = s % Y, s // Y
    core, cx, zh = t % CORES, (t // CORES) % X, t // (CORES * X)
    quad, place_z = zl // QUAD, zl % QUAD
    late = quad
    ready_x, ready_core, ready_y, ready_near, ready_cross, ready_far = (ready.at[n] for n in range(6))

    def tok_of(h, x, c):
        return h * (X * CORES) + x * CORES + c

    def block_of(h, x, c):
        return h * per_half + c * X + x

    def other_x(k):
        return (cx + k) % X

    far = (s, tok_of(1 - zh, cx, core))
    sibling = (s, tok_of(zh, cx, 1 - core))
    along_x = [(s, tok_of(zh, other_x(k), core)) for k in range(1, X)]
    along_y = [(zl * Y + (y + k) % Y, t) for k in range(1, Y)]
    in_quad = [((quad * QUAD + (place_z + k) % QUAD) * Y + y, t) for k in range(1, QUAD)]
    opposite_z = (1 - quad) * QUAD + place_z
    opposite = (opposite_z * Y + y, t)

    def signal(semaphore, who):
        pl.semaphore_signal(semaphore, inc=1, device_id=who, device_id_type=MESH)

    loads = [
        (x_hbm, x_raw, 0), (bias_hbm, bias_raw, 1), (chain_hbm, small.at[0], 2), (pad_hbm, small.at[1], 2),
        (gain_hbm, gain_s, 3), (wq_hbm, weights.at[0], 4), (wk_hbm, weights.at[1], 5), (wv_hbm, weights.at[2], 5),
        (wo_hbm, weights.at[3], 6),
    ]
    for src, dst, n in loads:
        pltpu.make_async_copy(src, dst, lsem.at[n]).start()

    barrier = pltpu.get_barrier_semaphore()

    @pl.when(zh == 0)
    def _():
        signal(barrier, far)

    @pl.when(core == CORES - 1)
    def _():
        signal(barrier, sibling)

    for k in range(1, X):

        @pl.when(cx + k < X)
        def _(k=k):
            signal(barrier, along_x[k - 1])

    for k in range(1, Y):

        @pl.when(y + k < Y)
        def _(k=k):
            signal(barrier, along_y[k - 1])

    for k in range(1, QUAD):

        @pl.when(place_z + k < QUAD)
        def _(k=k):
            signal(barrier, in_quad[k - 1])

    @pl.when(late == 0)
    def _():
        signal(barrier, opposite)

    def loaded(ref, n):
        pltpu.make_async_copy(ref, ref, lsem.at[n]).wait()

    def remote(ref, send, recv, who):
        return pltpu.make_async_remote_copy(
            src_ref=ref, dst_ref=ref, send_sem=send, recv_sem=recv, device_id=who, device_id_type=MESH
        )

    FAR = X

    def send_x(block, n, who, piece=slice(None)):
        remote(xbuf.at[block, piece], xs, xr.at[n], who).start()

    def recv_x(blocks, n):
        remote(blocks, xs, xr.at[n], sibling).wait_recv()

    def send_z(n, who, there):
        remote(bbuf.at[there, y], bzs, bzr.at[n], who).start()

    def recv_z(blocks, n):
        remote(blocks, bzs, bzr.at[n], sibling).wait_recv()

    def hand_on_y(blocks):
        for who in along_y:
            remote(blocks, bys, byr, who).start()

    PIECES = 2
    pieces = [pl.ds(p * (rows // PIECES), rows // PIECES) for p in range(PIECES)]

    def send_far():
        for p, piece in enumerate(pieces):
            pltpu.make_async_remote_copy(
                src_ref=x_raw.at[0, piece], dst_ref=far_raw.at[0, piece], send_sem=xs, recv_sem=xr.at[FAR + X * p],
                device_id=far, device_id_type=MESH,
            ).start()

    earlier = zh + (CORES - 1 - core) + cx + y + place_z + late

    @pl.when(earlier > 0)
    def _():
        pl.semaphore_wait(barrier, earlier)

    loaded(x_raw, 0)

    @pl.when(zh == 1)
    def _():
        signal(ready_far, far)
        send_far()

    own = block_of(zh, cx, core)

    loaded(bias_raw, 1)
    bbuf[zl, y] = jnp.concatenate([bias_raw[h] for h in range(heads)], axis=1)

    for k in range(1, Y):

        @pl.when(y + k >= Y)
        def _(k=k):
            signal(ready_y, along_y[k - 1])

    for k in range(1, QUAD):

        @pl.when(place_z + k >= QUAD)
        def _(k=k):
            signal(ready_near, in_quad[k - 1])
            send_z(0, in_quad[k - 1], zl)

    @pl.when(late == 1)
    def _():
        signal(ready_cross, opposite)
        send_z(1, opposite, zl)

    xbuf[own] = layer_norm(x_raw[0])


    for k in range(1, X):

        @pl.when(cx + k >= X)
        def _(k=k):
            signal(ready_x, along_x[k - 1])
            send_x(own, X - k, along_x[k - 1])

    @pl.when(core == 0)
    def _():
        signal(ready_core, sibling)
        send_x(own, 0, sibling)

    @pl.when(cx < X - 1)
    def _():
        pl.semaphore_wait(ready_x, X - 1 - cx)

    for k in range(1, X):

        @pl.when(cx + k < X)
        def _(k=k):
            send_x(own, X - k, along_x[k - 1])

    @pl.when(place_z < QUAD - 1)
    def _():
        pl.semaphore_wait(ready_near, QUAD - 1 - place_z)

    for k in range(1, QUAD):

        @pl.when(place_z + k < QUAD)
        def _(k=k):
            send_z(0, in_quad[k - 1], zl)

    @pl.when(late == 0)
    def _():
        pl.semaphore_wait(ready_cross, 1)
        send_z(1, opposite, zl)

    @pl.when(core == CORES - 1)
    def _():
        pl.semaphore_wait(ready_core, 1)
        send_x(own, 0, sibling)

    loaded(small, 2)
    tokens = small.shape[1]
    chain_row = small[0:1].astype(F32)
    chain_col[...] = jnp.transpose(jnp.broadcast_to(chain_row, (128, tokens))).reshape(chain_col.shape)
    mask_row = (small[1:2].astype(F32) - 1.0) * 1000000000.0
    mask_col[...] = jnp.transpose(jnp.broadcast_to(mask_row, (128, tokens))).reshape(mask_col.shape)
    lane = lax.broadcasted_iota(jnp.int32, (rows, lanes), 1)
    query = lax.broadcasted_iota(jnp.int32, (rows, lanes), 0)
    pick = lane % rows == query
    own_chain = chain_col[t // CORES, core][:, 0:1]
    query_chain = jnp.sum(jnp.where(pick, own_chain, 0.0), axis=0, keepdims=True)
    loaded(gain_s, 3)
    gain = jnp.zeros((1, lanes), F32)
    lane_head = lax.broadcasted_iota(jnp.int32, (1, lanes), 1) // rows
    for h in range(heads):
        gain = jnp.where(lane_head == h, gain_s[h], gain)

    loaded(weights.at[0], 4)
    queries = dot(xbuf[own], weights[0]).astype(BF16)
    group_heads = heads // 2
    group_width = width // 2
    group_lanes = lanes // 2
    row_head = lax.broadcasted_iota(jnp.int32, (group_lanes, group_width), 0) // rows
    col_head = lax.broadcasted_iota(jnp.int32, (group_lanes, group_width), 1) // head_size
    for g in range(2):
        part = queries[:, g * group_width : (g + 1) * group_width]
        tiled = jnp.concatenate([part] * group_heads, axis=0)
        qexp[g] = jnp.where(row_head == col_head, tiled, jnp.zeros_like(tiled))

    loaded(weights.at[pl.ds(1, 2)], 5)

    def values(first, count):
        block = xbuf[pl.ds(first, count // rows)].reshape(count, width)
        return jnp.transpose(dot(block, weights[2]).astype(BF16))

    def raw_scores(h, c):
        block = xbuf[pl.ds(block_of(h, 0, c), X)].reshape(quarter, width)
        key = dot(block, weights[1]).astype(BF16)
        return jnp.concatenate(
            [dot_t(key[:, g * group_width : (g + 1) * group_width], qexp[g]) for g in range(2)], axis=1
        )

    def scores(found, at, h, c):
        bias = bbuf[pl.ds(h * QUAD, QUAD), pl.ds(c * (Y // CORES), Y // CORES)].reshape(quarter, lanes).astype(F32)
        key_chain = chain_col[pl.ds(h * X, X), c].reshape(quarter, 128)[:, 0:1]
        key_mask = mask_col[pl.ds(h * X, X), c].reshape(quarter, 128)[:, 0:1]
        found = found * (1.0 / math.sqrt(head_size)) + bias
        found = found + jnp.where(key_chain == query_chain, gain, 0.0)
        found = found + key_mask
        top = jnp.max(found, axis=0, keepdims=True)
        expo = jnp.exp(found - top)
        ebuf[at] = expo
        return at, top, jnp.sum(expo, axis=0, keepdims=True)

    def part_of(c):
        return pl.ds(pl.multiple_of(half + c * quarter, quarter), quarter)

    for k in range(1, X):
        block = block_of(zh, other_x(k), core)
        recv_x(xbuf.at[block], k)
        send_x(block, 0, sibling)

    recv_z(bbuf.at[opposite_z, y], 1)
    for k in range(1, QUAD):
        send_z(1 + QUAD - k, in_quad[k - 1], opposite_z)

    @pl.when(y < Y - 1)
    def _():
        pl.semaphore_wait(ready_y, Y - 1 - y)

    hand_on_y(bbuf.at[opposite_z, y])

    recv_z(bbuf.at[pl.ds(0, QUAD - 1), y], 0)

    hand_on_y(bbuf.at[pl.ds(quad * QUAD, QUAD), y])

    @pl.when((zh == 0) & (zl > 0))
    def _():
        pl.semaphore_wait(ready_far, 1)
        send_far()

    recv_x(xbuf.at[pl.ds(0, X)], 0)
    vbuf[:, 0:half] = values(zh * per_half, half)
    for c in range(CORES):
        ebuf[c * quarter : (c + 1) * quarter] = raw_scores(zh, c)

    far_block = block_of(1 - zh, cx, core)

    def cross_step():
        for k in range(1, QUAD):
            there = (1 - quad) * QUAD + (place_z + k) % QUAD
            recv_z(bbuf.at[there, y], 1 + k)
            hand_on_y(bbuf.at[there, y])

    def far_step():
        for p, piece in enumerate(pieces):
            recv_x(far_raw.at[0, piece], FAR + X * p)
            xbuf[far_block, piece] = layer_norm(far_raw[0, piece])
            for k in (2, 1, 3):
                send_x(far_block, FAR + X * p + X - k, along_x[k - 1], piece)
            send_x(far_block, FAR + X * PIECES, sibling, piece)

    @pl.when(late == 0)
    def _():
        cross_step()
        far_step()

        @pl.when((zh == 0) & (zl == 0))
        def _():
            pl.semaphore_wait(ready_far, 1)
            send_far()

    @pl.when(late == 1)
    def _():
        far_step()
        cross_step()

    for p, piece in enumerate(pieces):
        for k in (1, 3, 2):
            block = block_of(1 - zh, other_x(k), core)
            recv_x(xbuf.at[block, piece], FAR + X * p + k)
            send_x(block, FAR + X * PIECES, sibling, piece)

    raw = raw_scores(1 - zh, core)
    vbuf[:, part_of(core)] = values(block_of(1 - zh, 0, core), quarter)
    remote(bbuf.at[pl.ds(0, 2 * (Y - 1))], bys, byr, sibling).wait_recv()
    found = []
    for c in range(CORES):
        at = pl.ds(c * quarter, quarter)
        found.append(scores(ebuf[at], at, zh, c))
    found.append(scores(raw, part_of(core), 1 - zh, core))
    recv_x(xbuf.at[pl.ds(0, X)], FAR + X * PIECES)
    found.append(scores(raw_scores(1 - zh, 1 - core), part_of(1 - core), 1 - zh, 1 - core))
    vbuf[:, part_of(1 - core)] = values(block_of(1 - zh, 0, 1 - core), quarter)

    top = functools.reduce(jnp.maximum, [f[1] for f in found])
    shares = [jnp.exp(f[1] - top) for f in found]
    total = sum(f[2] * share for f, share in zip(found, shares))
    for (at, _, _), share in zip(found, shares):
        wbuf[at] = (ebuf[at] * (share / total)).astype(BF16)

    feature_head = lax.broadcasted_iota(jnp.int32, (group_width, group_lanes), 0) // head_size
    lane_of = lax.broadcasted_iota(jnp.int32, (group_width, group_lanes), 1) // rows
    place = pick[:, :group_lanes].astype(BF16)
    kept = []
    for g in range(2):
        f = slice(g * group_width, (g + 1) * group_width)
        l = slice(g * group_lanes, (g + 1) * group_lanes)
        kept.append(jnp.where(feature_head == lane_of, dot(vbuf[f], wbuf[:, l]), 0.0).astype(BF16))
    attended = dot_t(place, jnp.concatenate(kept, axis=0)).astype(BF16)

    loaded(weights.at[3], 6)
    projected = dot(attended, weights[3])
    ratio = jnp.full((1, width), step_s[0], jnp.int32).astype(F32) / (STEPS - 1)
    upper, lower = SIGMA_TOP ** (1.0 / RHO), SIGMA_LOW ** (1.0 / RHO)
    base = upper + ratio * (lower - upper)
    square = base * base
    sigma = SIGMA_DATA * (square * square * square * base)
    skip_scale = SIGMA_DATA**2 / (SIGMA_DATA**2 + sigma * sigma)
    out_scale = sigma / jnp.sqrt(sigma * sigma + SIGMA_DATA**2)
    out_ref[0] = (skip_scale * x_raw[0].astype(F32) + out_scale * projected).astype(BF16)

    remote(xbuf.at[pl.ds(0, 4 * X - 1)], xs, xr.at[0], sibling).wait_send()
    remote(bbuf.at[pl.ds(0, 2 * QUAD - 1), y], bzs, bzr.at[0], sibling).wait_send()
    remote(bbuf.at[pl.ds(0, 2 * (Y - 1))], bys, byr, sibling).wait_send()


def shards(noisy, pair_bias, chain_ids, pad_mask, step_index, chain_gain, w_query, w_key, w_value, w_output):
    samples, rows, width = noisy.shape
    heads, _, keys_each = pair_bias.shape
    tokens = chain_ids.shape[0]
    blocks = tokens // rows
    lanes = heads * rows
    dma = pltpu.SemaphoreType.DMA
    column = pltpu.VMEM((blocks // CORES, CORES, rows, 128), F32)
    large = [
        noisy, jnp.transpose(pair_bias, (0, 2, 1)), chain_ids, pad_mask, chain_gain,
        w_query, w_key, w_value, w_output,
    ]
    return pl.pallas_call(
        kernel,
        out_shape=jax.ShapeDtypeStruct((samples, rows, width), BF16),
        in_specs=[pl.BlockSpec(memory_space=pltpu.SMEM)] + [pl.BlockSpec(memory_space=pltpu.HBM)] * len(large),
        out_specs=pl.BlockSpec(memory_space=pltpu.VMEM),
        scratch_shapes=[
            pltpu.VMEM((samples, rows, width), BF16),
            pltpu.VMEM((samples, rows, width), BF16),
            pltpu.VMEM((heads, keys_each, rows), BF16),
            pltpu.VMEM((2, tokens), jnp.int32),
            pltpu.SMEM((heads,), F32),
            pltpu.VMEM((4, width, width), BF16),
            pltpu.VMEM((blocks, rows, width), BF16),
            pltpu.VMEM((Z_LO, Y, keys_each, lanes), BF16),
            pltpu.VMEM((width, tokens), BF16),
            pltpu.VMEM((2, lanes // 2, width // 2), BF16),
            pltpu.VMEM((tokens, lanes), F32),
            pltpu.VMEM((tokens, lanes), BF16),
            column, column,
            dma((7,)),
            dma,
            dma((3 * X + 1,)),
            dma,
            dma((1 + QUAD,)),
            dma,
            dma,
            pltpu.SemaphoreType.REGULAR((6,)),
        ],
        compiler_params=pltpu.CompilerParams(
            collective_id=0, has_side_effects=True, vmem_limit_bytes=32 * 1024 * 1024
        ),
    )(step_index, *[pltpu.with_memory_space_constraint(a, pltpu.HBM) for a in large])


def solution(mesh):
    in_specs = (
        P("sample", "tok", None),
        P(None, "tok", "sample"),
        P(),
        P(),
        P("sample"),
        P(),
        P(),
        P(),
        P(),
        P(),
    )
    out_specs = P("sample", "tok", None)
    return jax.shard_map(shards, mesh=mesh, in_specs=in_specs, out_specs=out_specs, check_vma=False)
```

```python
import functools
import math

import jax
import jax.numpy as jnp
from jax import lax
from jax.experimental import pallas as pl
from jax.experimental.pallas import tpu as pltpu
from jax.sharding import PartitionSpec as P

STEPS = 200
SIGMA_DATA = 16.0
SIGMA_TOP = 160.0
SIGMA_LOW = 0.0004
RHO = 7

Y, Z_LO = 4, 8
X, CORES = 4, 2

MESH = pl.DeviceIdType.MESH
F32 = jnp.float32
BF16 = jnp.bfloat16
QUAD = Z_LO // 2


def layer_norm(values):
    xf = values.astype(F32)
    center = xf - jnp.mean(xf, axis=-1, keepdims=True)
    spread = jnp.mean(center * center, axis=-1, keepdims=True)
    return (center * lax.rsqrt(spread + 1e-05)).astype(BF16)


def dot(a, b):
    return lax.dot_general(a, b, (((1,), (0,)), ((), ())), preferred_element_type=F32)


def dot_t(a, b):
    return lax.dot_general(a, b, (((1,), (1,)), ((), ())), preferred_element_type=F32)


def kernel(
    step_s, x_hbm, bias_hbm, chain_hbm, pad_hbm, gain_hbm, wq_hbm, wk_hbm, wv_hbm, wo_hbm,
    out_ref,
    x_raw, far_raw, bias_raw, small, gain_s, weights,
    xbuf, bbuf, vbuf, qexp, ebuf, wbuf, chain_col, mask_col,
    lsem, xs, xr, bzs, bzr, bys, byr, ready,
):
    heads, keys_each, rows = bias_hbm.shape
    width = x_hbm.shape[2]
    per_half = xbuf.shape[0] // 2
    half = per_half * rows
    quarter = half // CORES
    head_size = width // heads
    lanes = heads * rows

    s, t = lax.axis_index("sample"), lax.axis_index("tok")
    y, zl = s % Y, s // Y
    core, cx, zh = t % CORES, (t // CORES) % X, t // (CORES * X)
    quad, place_z = zl // QUAD, zl % QUAD
    late = (quad + zh * (place_z // 2)) % 2
    ready_x, ready_core, ready_y, ready_near, ready_cross, ready_far = (ready.at[n] for n in range(6))

    def tok_of(h, x, c):
        return h * (X * CORES) + x * CORES + c

    def block_of(h, x, c):
        return h * per_half + c * X + x

    def other_x(k):
        return (cx + k) % X

    far = (s, tok_of(1 - zh, cx, core))
    sibling = (s, tok_of(zh, cx, 1 - core))
    along_x = [(s, tok_of(zh, other_x(k), core)) for k in range(1, X)]
    along_y = [(zl * Y + (y + k) % Y, t) for k in range(1, Y)]
    in_quad = [((quad * QUAD + (place_z + k) % QUAD) * Y + y, t) for k in range(1, QUAD)]
    opposite_z = (1 - quad) * QUAD + place_z
    opposite = (opposite_z * Y + y, t)

    def signal(semaphore, who):
        pl.semaphore_signal(semaphore, inc=1, device_id=who, device_id_type=MESH)

    barrier = pltpu.get_barrier_semaphore()

    @pl.when(zh == 0)
    def _():
        signal(barrier, far)

    @pl.when(core == CORES - 1)
    def _():
        signal(barrier, sibling)

    for k in range(1, X):

        @pl.when(cx + k < X)
        def _(k=k):
            signal(barrier, along_x[k - 1])

    for k in range(1, Y):

        @pl.when(y + k < Y)
        def _(k=k):
            signal(barrier, along_y[k - 1])

    for k in range(1, QUAD):

        @pl.when(place_z + k < QUAD)
        def _(k=k):
            signal(barrier, in_quad[k - 1])

    @pl.when(late == 0)
    def _():
        signal(barrier, opposite)

    loads = [
        (x_hbm, x_raw, 0), (bias_hbm, bias_raw, 1), (chain_hbm, small.at[0], 2), (pad_hbm, small.at[1], 2),
        (gain_hbm, gain_s, 3), (wq_hbm, weights.at[0], 4), (wk_hbm, weights.at[1], 4), (wv_hbm, weights.at[2], 4),
        (wo_hbm, weights.at[3], 4),
    ]
    for src, dst, n in loads:
        pltpu.make_async_copy(src, dst, lsem.at[n]).start()

    def loaded(ref, n):
        pltpu.make_async_copy(ref, ref, lsem.at[n]).wait()

    def remote(ref, send, recv, who):
        return pltpu.make_async_remote_copy(
            src_ref=ref, dst_ref=ref, send_sem=send, recv_sem=recv, device_id=who, device_id_type=MESH
        )

    FAR = 2

    def send_x(block, n, who, piece=slice(None)):
        remote(xbuf.at[block, piece], xs, xr.at[n], who).start()

    def recv_x(blocks, n):
        remote(blocks, xs, xr.at[n], sibling).wait_recv()

    def send_z(n, who, there):
        remote(bbuf.at[there, y], bzs, bzr.at[n], who).start()

    def recv_z(blocks, n):
        remote(blocks, bzs, bzr.at[n], sibling).wait_recv()

    def hand_on_y(blocks):
        for who in along_y:
            remote(blocks, bys, byr, who).start()

    PIECES = 2
    pieces = [pl.ds(p * (rows // PIECES), rows // PIECES) for p in range(PIECES)]

    def send_far():
        for p, piece in enumerate(pieces):
            pltpu.make_async_remote_copy(
                src_ref=x_raw.at[0, piece], dst_ref=far_raw.at[0, piece], send_sem=xs, recv_sem=xr.at[FAR + X * p],
                device_id=far, device_id_type=MESH,
            ).start()

    earlier = zh + (CORES - 1 - core) + cx + y + place_z + late

    @pl.when(earlier > 0)
    def _():
        pl.semaphore_wait(barrier, earlier)

    loaded(x_raw, 0)

    @pl.when(zh == 1)
    def _():
        signal(ready_far, far)
        send_far()

    own = block_of(zh, cx, core)

    loaded(bias_raw, 1)
    bbuf[zl, y] = jnp.concatenate([bias_raw[h] for h in range(heads)], axis=1)

    for k in range(1, Y):

        @pl.when(y + k >= Y)
        def _(k=k):
            signal(ready_y, along_y[k - 1])

    for k in range(1, QUAD):

        @pl.when(place_z + k >= QUAD)
        def _(k=k):
            signal(ready_near, in_quad[k - 1])
            send_z(0, in_quad[k - 1], zl)

    @pl.when(late == 1)
    def _():
        signal(ready_cross, opposite)
        send_z(1, opposite, zl)

    xbuf[own] = layer_norm(x_raw[0])


    for k in range(1, X):

        @pl.when(cx + k >= X)
        def _(k=k):
            signal(ready_x, along_x[k - 1])
            send_x(own, 1, along_x[k - 1])

    @pl.when(core == 0)
    def _():
        signal(ready_core, sibling)
        send_x(own, 0, sibling)

    @pl.when(cx < X - 1)
    def _():
        pl.semaphore_wait(ready_x, X - 1 - cx)

    for k in range(1, X):

        @pl.when(cx + k < X)
        def _(k=k):
            send_x(own, 1, along_x[k - 1])

    @pl.when(place_z < QUAD - 1)
    def _():
        pl.semaphore_wait(ready_near, QUAD - 1 - place_z)

    for k in range(1, QUAD):

        @pl.when(place_z + k < QUAD)
        def _(k=k):
            send_z(0, in_quad[k - 1], zl)

    @pl.when(late == 0)
    def _():
        pl.semaphore_wait(ready_cross, 1)
        send_z(1, opposite, zl)

    @pl.when(core == CORES - 1)
    def _():
        pl.semaphore_wait(ready_core, 1)
        send_x(own, 0, sibling)

    loaded(small, 2)
    tokens = small.shape[1]
    chain_row = small[0:1].astype(F32)
    chain_col[...] = jnp.transpose(jnp.broadcast_to(chain_row, (128, tokens))).reshape(chain_col.shape)
    mask_row = (small[1:2].astype(F32) - 1.0) * 1000000000.0
    mask_col[...] = jnp.transpose(jnp.broadcast_to(mask_row, (128, tokens))).reshape(mask_col.shape)
    lane = lax.broadcasted_iota(jnp.int32, (rows, lanes), 1)
    query = lax.broadcasted_iota(jnp.int32, (rows, lanes), 0)
    pick = lane % rows == query
    own_chain = chain_col[t // CORES, core][:, 0:1]
    query_chain = jnp.sum(jnp.where(pick, own_chain, 0.0), axis=0, keepdims=True)
    loaded(gain_s, 3)
    gain = jnp.zeros((1, lanes), F32)
    lane_head = lax.broadcasted_iota(jnp.int32, (1, lanes), 1) // rows
    for h in range(heads):
        gain = jnp.where(lane_head == h, gain_s[h], gain)

    loaded(weights, 4)
    queries = dot(xbuf[own], weights[0]).astype(BF16)
    group_heads = heads // 2
    group_width = width // 2
    group_lanes = lanes // 2
    row_head = lax.broadcasted_iota(jnp.int32, (group_lanes, group_width), 0) // rows
    col_head = lax.broadcasted_iota(jnp.int32, (group_lanes, group_width), 1) // head_size
    for g in range(2):
        part = queries[:, g * group_width : (g + 1) * group_width]
        tiled = jnp.concatenate([part] * group_heads, axis=0)
        qexp[g] = jnp.where(row_head == col_head, tiled, jnp.zeros_like(tiled))


    def values(first, count):
        block = xbuf[pl.ds(first, count // rows)].reshape(count, width)
        return jnp.transpose(dot(block, weights[2]).astype(BF16))

    def raw_scores(h, c):
        block = xbuf[pl.ds(block_of(h, 0, c), X)].reshape(quarter, width)
        key = dot(block, weights[1]).astype(BF16)
        return jnp.concatenate(
            [dot_t(key[:, g * group_width : (g + 1) * group_width], qexp[g]) for g in range(2)], axis=1
        )

    def scores(found, at, h, c):
        bias = bbuf[pl.ds(h * QUAD, QUAD), pl.ds(c * (Y // CORES), Y // CORES)].reshape(quarter, lanes).astype(F32)
        key_chain = chain_col[pl.ds(h * X, X), c].reshape(quarter, 128)[:, 0:1]
        key_mask = mask_col[pl.ds(h * X, X), c].reshape(quarter, 128)[:, 0:1]
        found = found * (1.0 / math.sqrt(head_size)) + bias
        found = found + jnp.where(key_chain == query_chain, gain, 0.0)
        found = found + key_mask
        top = jnp.max(found, axis=0, keepdims=True)
        expo = jnp.exp(found - top)
        ebuf[at] = expo
        return at, top, jnp.sum(expo, axis=0, keepdims=True)

    def part_of(c):
        return pl.ds(pl.multiple_of(half + c * quarter, quarter), quarter)

    recv_x(xbuf.at[pl.ds(0, X - 1)], 1)
    for k in range(1, X):
        send_x(block_of(zh, other_x(k), core), 0, sibling)

    recv_z(bbuf.at[opposite_z, y], 1)
    for k in range(1, QUAD):
        send_z(1 + QUAD - k, in_quad[k - 1], opposite_z)

    @pl.when(y < Y - 1)
    def _():
        pl.semaphore_wait(ready_y, Y - 1 - y)

    hand_on_y(bbuf.at[opposite_z, y])

    recv_z(bbuf.at[pl.ds(0, QUAD - 1), y], 0)

    hand_on_y(bbuf.at[pl.ds(quad * QUAD, QUAD), y])

    @pl.when((zh == 0) & (zl > 0))
    def _():
        pl.semaphore_wait(ready_far, 1)
        send_far()

    recv_x(xbuf.at[pl.ds(0, X)], 0)
    vbuf[:, 0:half] = values(zh * per_half, half)
    for c in range(CORES):
        ebuf[c * quarter : (c + 1) * quarter] = raw_scores(zh, c)

    far_block = block_of(1 - zh, cx, core)

    def cross_step():
        for k in range(1, QUAD):
            there = (1 - quad) * QUAD + (place_z + k) % QUAD
            recv_z(bbuf.at[there, y], 1 + k)
            hand_on_y(bbuf.at[there, y])

    def far_step():
        for p, piece in enumerate(pieces):
            recv_x(far_raw.at[0, piece], FAR + X * p)
            xbuf[far_block, piece] = layer_norm(far_raw[0, piece])
            for k in (2, 1, 3):
                send_x(far_block, FAR + X * p + X - k, along_x[k - 1], piece)
            send_x(far_block, FAR + X * PIECES, sibling, piece)

    @pl.when(late == 0)
    def _():
        cross_step()
        far_step()

        @pl.when((zh == 0) & (zl == 0))
        def _():
            pl.semaphore_wait(ready_far, 1)
            send_far()

    @pl.when(late == 1)
    def _():
        far_step()
        cross_step()

    for p, piece in enumerate(pieces):
        for k in (1, 3, 2):
            block = block_of(1 - zh, other_x(k), core)
            recv_x(xbuf.at[block, piece], FAR + X * p + k)
            send_x(block, FAR + X * PIECES, sibling, piece)

    remote(bbuf.at[pl.ds(0, 2 * (Y - 1))], bys, byr, sibling).wait_recv()
    found = []
    for c in range(CORES):
        at = pl.ds(c * quarter, quarter)
        found.append(scores(ebuf[at], at, zh, c))
    found.append(scores(raw_scores(1 - zh, core), part_of(core), 1 - zh, core))
    vbuf[:, part_of(core)] = values(block_of(1 - zh, 0, core), quarter)
    recv_x(xbuf.at[pl.ds(0, X)], FAR + X * PIECES)
    found.append(scores(raw_scores(1 - zh, 1 - core), part_of(1 - core), 1 - zh, 1 - core))
    vbuf[:, part_of(1 - core)] = values(block_of(1 - zh, 0, 1 - core), quarter)

    top = functools.reduce(jnp.maximum, [f[1] for f in found])
    shares = [jnp.exp(f[1] - top) for f in found]
    total = sum(f[2] * share for f, share in zip(found, shares))
    for (at, _, _), share in zip(found, shares):
        wbuf[at] = (ebuf[at] * (share / total)).astype(BF16)

    feature_head = lax.broadcasted_iota(jnp.int32, (group_width, group_lanes), 0) // head_size
    lane_of = lax.broadcasted_iota(jnp.int32, (group_width, group_lanes), 1) // rows
    place = pick[:, :group_lanes].astype(BF16)
    kept = []
    for g in range(2):
        f = slice(g * group_width, (g + 1) * group_width)
        l = slice(g * group_lanes, (g + 1) * group_lanes)
        kept.append(jnp.where(feature_head == lane_of, dot(vbuf[f], wbuf[:, l]), 0.0).astype(BF16))
    attended = dot_t(place, jnp.concatenate(kept, axis=0)).astype(BF16)

    projected = dot(attended, weights[3])
    ratio = jnp.full((1, width), step_s[0], jnp.int32).astype(F32) / (STEPS - 1)
    upper, lower = SIGMA_TOP ** (1.0 / RHO), SIGMA_LOW ** (1.0 / RHO)
    base = upper + ratio * (lower - upper)
    square = base * base
    sigma = SIGMA_DATA * (square * square * square * base)
    skip_scale = SIGMA_DATA**2 / (SIGMA_DATA**2 + sigma * sigma)
    out_scale = sigma / jnp.sqrt(sigma * sigma + SIGMA_DATA**2)
    out_ref[0] = (skip_scale * x_raw[0].astype(F32) + out_scale * projected).astype(BF16)

    remote(xbuf.at[pl.ds(0, 4 * X - 1)], xs, xr.at[0], sibling).wait_send()
    remote(bbuf.at[pl.ds(0, 2 * QUAD - 1), y], bzs, bzr.at[0], sibling).wait_send()
    remote(bbuf.at[pl.ds(0, 2 * (Y - 1))], bys, byr, sibling).wait_send()


def shards(noisy, pair_bias, chain_ids, pad_mask, step_index, chain_gain, w_query, w_key, w_value, w_output):
    samples, rows, width = noisy.shape
    heads, _, keys_each = pair_bias.shape
    tokens = chain_ids.shape[0]
    blocks = tokens // rows
    lanes = heads * rows
    dma = pltpu.SemaphoreType.DMA
    column = pltpu.VMEM((blocks // CORES, CORES, rows, 128), F32)
    large = [
        noisy, jnp.transpose(pair_bias, (0, 2, 1)), chain_ids, pad_mask, chain_gain,
        w_query, w_key, w_value, w_output,
    ]
    return pl.pallas_call(
        kernel,
        out_shape=jax.ShapeDtypeStruct((samples, rows, width), BF16),
        in_specs=[pl.BlockSpec(memory_space=pltpu.SMEM)] + [pl.BlockSpec(memory_space=pltpu.HBM)] * len(large),
        out_specs=pl.BlockSpec(memory_space=pltpu.VMEM),
        scratch_shapes=[
            pltpu.VMEM((samples, rows, width), BF16),
            pltpu.VMEM((samples, rows, width), BF16),
            pltpu.VMEM((heads, keys_each, rows), BF16),
            pltpu.VMEM((2, tokens), jnp.int32),
            pltpu.SMEM((heads,), F32),
            pltpu.VMEM((4, width, width), BF16),
            pltpu.VMEM((blocks, rows, width), BF16),
            pltpu.VMEM((Z_LO, Y, keys_each, lanes), BF16),
            pltpu.VMEM((width, tokens), BF16),
            pltpu.VMEM((2, lanes // 2, width // 2), BF16),
            pltpu.VMEM((tokens, lanes), F32),
            pltpu.VMEM((tokens, lanes), BF16),
            column, column,
            dma((5,)),
            dma,
            dma((2 * X + 3,)),
            dma,
            dma((1 + QUAD,)),
            dma,
            dma,
            pltpu.SemaphoreType.REGULAR((6,)),
        ],
        compiler_params=pltpu.CompilerParams(
            collective_id=0, has_side_effects=True, vmem_limit_bytes=32 * 1024 * 1024
        ),
    )(step_index, *[pltpu.with_memory_space_constraint(a, pltpu.HBM) for a in large])


def solution(mesh):
    in_specs = (
        P("sample", "tok", None),
        P(None, "tok", "sample"),
        P(),
        P(),
        P("sample"),
        P(),
        P(),
        P(),
        P(),
        P(),
    )
    out_specs = P("sample", "tok", None)
    return jax.shard_map(shards, mesh=mesh, in_specs=in_specs, out_specs=out_specs, check_vma=False)
```
